32 devices in a mesh: seq: 8 (over z, x), doc: 4 (over y, core).
Axes of the slice: x: 2, y: 2, z: 4, core: 2. Of those that a mesh axis runs over, the one named last changes fastest.
Arguments:
- queries: bfloat16 [4096, 2048], P(('doc', 'seq')), parts along dimension 0, may hold values from -5 to 5
- key_rows: bfloat16 [4096, 2048], P(('doc', 'seq')), parts along dimension 0, may hold values from -5 to 5
- value_rows: bfloat16 [4096, 2048], P(('doc', 'seq')), parts along dimension 0, may hold values from -6 to 6
- out_grad: bfloat16 [4096, 2048], P(('doc', 'seq')), parts along dimension 0, may hold values from -6 to 6
- vertical: int32 [64, 6], P('doc'), parts along dimension 0, may hold values from 0 to 7, as said below
- slash_offsets: int32 [64, 6], P('doc'), parts along dimension 0, may hold values from -7 to 7, as said below
- counts: int32 [64, 2], P('doc'), parts along dimension 0, may hold values from 1 to 6, as said below
Outputs:
- query_grad: bfloat16 [4096, 2048], P(('doc', 'seq')), parts along dimension 0
- key_grad: bfloat16 [4096, 2048], P(('doc', 'seq')), parts along dimension 0
- value_grad: bfloat16 [4096, 2048], P(('doc', 'seq')), parts along dimension 0
The draws below stay inside these ranges and needn't reach their ends.
There are 4 independent parts, one for each index of `doc`. The reference program is written for one: setup_inputs(seed, part) draws one part's arguments, and reference() takes and returns one part's arrays. A program takes and returns all parts, laid end to end along the dimension named above; each array names one. Nothing has to cross between parts.
Inputs may be any that keep to these rules, and one draw needn't show every extreme that they name: counts[h, 0] is 1 to 6 and counts[h, 1] is 1 to 6; some head has both at their most and some head both at 1. `vertical`: the entries of a head are distinct. `slash_offsets`: the entries of a head are distinct and slash_offsets[h, 0] is 0 for every head.
All inputs are finite; a program needn't handle non-finite values.
Results may differ from the reference program's by a relative error of at most 0.0086.
Values may be sent and summed in bfloat16 or wider, within the bound.
A program may use at most 64 MiB of HBM per device.

```python
import jax
import jax.numpy as jnp
from jax import lax

HEADS = 16
HEAD_DIM = 128
BLK = 128
NV = 6
NS = 6
SEQ_LEN = 1024
BLOCKS = 8


def draw_queries(key, part):
    base = jnp.clip(jax.random.normal(jax.random.fold_in(key, 1), (SEQ_LEN, HEADS * HEAD_DIM)), -4.0, 4.0)
    return base.astype(jnp.bfloat16)


def draw_key_rows(key, part):
    base = jnp.clip(jax.random.normal(jax.random.fold_in(key, 4), (SEQ_LEN, HEADS * HEAD_DIM)), -4.0, 4.0)
    return base.astype(jnp.bfloat16)


def draw_counts(key, part):

    def skewed(base_key, most):
        first_pick = jax.random.randint(jax.random.fold_in(base_key, 0), (HEADS,), 1, most + 1)
        second_pick = jax.random.randint(jax.random.fold_in(base_key, 1), (HEADS,), 1, most + 1)
        return jnp.minimum(first_pick, second_pick)
    vert_count = skewed(jax.random.fold_in(key, 21), NV)
    slash_count = skewed(jax.random.fold_in(key, 22), NS)
    order = jax.random.permutation(jax.random.fold_in(key, 23), HEADS)
    head_ids = jnp.arange(HEADS)
    vert_count = jnp.where(head_ids == order[0], NV, jnp.where(head_ids == order[1], 1, vert_count))
    slash_count = jnp.where(head_ids == order[0], NS, jnp.where(head_ids == order[1], 1, slash_count))
    return jnp.stack([vert_count, slash_count], axis=1).astype(jnp.int32)


def draw_vertical(key, part):
    head_keys = jax.random.split(jax.random.fold_in(key, 31), HEADS)
    picked = jax.vmap(lambda head_key: jax.random.permutation(head_key, BLOCKS)[:NV])(head_keys)
    return picked.astype(jnp.int32)


def draw_slash_offsets(key, part):
    head_keys = jax.random.split(jax.random.fold_in(key, 41), HEADS)
    sizes_drawn = jax.vmap(lambda head_key: jax.random.permutation(head_key, BLOCKS - 1)[:NS - 1] + 1)(head_keys)
    signs = jax.random.randint(jax.random.fold_in(key, 42), (HEADS, NS - 1), 0, 2) * 2 - 1
    offsets = jnp.concatenate([jnp.zeros((HEADS, 1), jnp.int32), (sizes_drawn * signs).astype(jnp.int32)], axis=1)
    return offsets.astype(jnp.int32)


def block_levels(own_key, shape, pieces, smallest, top_value):
    def one(dim, shards_of):
        draws = jax.random.uniform(jax.random.fold_in(jax.random.fold_in(own_key, 6), dim), (shards_of,), jnp.float32, smallest / len(pieces), top_value / len(pieces))
        return jnp.repeat(jnp.exp(draws), shape[dim] // shards_of).reshape((-1,) + (1,) * (len(shape) - dim - 1))

    factor_of = one(*pieces[0])
    for cut in pieces[1:]:
        factor_of = factor_of * one(*cut)
    return factor_of


def normal_values(rng, shape, deviation, bound, cuts=(), held_as=jnp.bfloat16):
    level = block_levels(rng, shape, cuts, -0.22, 0.18) if cuts else 1.0
    values = jax.random.normal(rng, shape, jnp.float32) * deviation * level
    return jnp.minimum(jnp.maximum(values, -bound), bound).astype(held_as)


def setup_inputs(seed: int = 0, part: int = 0) -> dict:
    key_of = jax.random.split(jax.random.key(seed), 8)
    part_splits = jax.random.split(jax.random.fold_in(key_of[7], part), 8)
    queries = draw_queries(jax.random.fold_in(jax.random.fold_in(key_of[7], part), 71), part)
    key_rows = draw_key_rows(jax.random.fold_in(jax.random.fold_in(key_of[7], part), 71), part)
    value_rows = normal_values(part_splits[2], (SEQ_LEN, HEADS * HEAD_DIM), 1.0, 6.0, ((0, 8),))
    out_grad = normal_values(part_splits[3], (SEQ_LEN, HEADS * HEAD_DIM), 1.0, 6.0, ((0, 8),))
    vertical = draw_vertical(jax.random.fold_in(jax.random.fold_in(key_of[7], part), 71), part)
    slash_offsets = draw_slash_offsets(jax.random.fold_in(jax.random.fold_in(key_of[7], part), 71), part)
    counts = draw_counts(jax.random.fold_in(jax.random.fold_in(key_of[7], part), 71), part)
    return dict(queries=queries, key_rows=key_rows, value_rows=value_rows, out_grad=out_grad, vertical=vertical, slash_offsets=slash_offsets, counts=counts)


block_group = 4


def block_lists(chosen, vert_head, slash_head, count_head, nblocks):
    vert_cap = vert_head.shape[0]
    slash_cap = slash_head.shape[0]
    rows_now = chosen.shape[0]
    vert_index = jnp.broadcast_to(vert_head[None, :], (rows_now, vert_cap))
    vert_valid = jnp.broadcast_to((jnp.arange(vert_cap, dtype=jnp.int32) < count_head[0])[None, :], (rows_now, vert_cap))
    slash_index = chosen[:, None] - slash_head[None, :]
    inside = (slash_index >= 0) & (slash_index < nblocks)
    repeated = jnp.any((vert_index[:, :, None] == slash_index[:, None, :]) & vert_valid[:, :, None], axis=1)
    slash_valid = (jnp.arange(slash_cap, dtype=jnp.int32) < count_head[1])[None, :] & inside & jnp.logical_not(repeated)
    index_table = jnp.clip(jnp.concatenate([vert_index, slash_index], axis=1), 0, nblocks - 1).astype(jnp.int32)
    valid_table = jnp.concatenate([vert_valid, slash_valid], axis=1)
    return index_table, valid_table


def head_reference(operands):
    q_blocks, k_blocks, v_blocks, d_blocks, vert_head, slash_head, count_head = operands
    nblocks, blk_rows, head_dim = q_blocks.shape
    score_scale = head_dim ** -0.5
    highest = lax.Precision.HIGHEST

    def one_group(carried, chosen):
        key_acc, value_acc = carried
        index_table, valid_table = block_lists(chosen, vert_head, slash_head, count_head, nblocks)
        groups_now, slot_count = index_table.shape
        q_group = q_blocks[chosen].astype(jnp.float32)
        d_group = d_blocks[chosen].astype(jnp.float32)
        k_tiles = k_blocks[index_table].reshape(groups_now, slot_count * blk_rows, head_dim).astype(jnp.float32)
        v_tiles = v_blocks[index_table].reshape(groups_now, slot_count * blk_rows, head_dim).astype(jnp.float32)
        allowed = jnp.repeat(valid_table, blk_rows, axis=1)[:, None, :]
        scores = jnp.einsum("gqd,gkd->gqk", q_group, k_tiles, precision=highest) * score_scale
        scores = jnp.where(allowed, scores, -1e30)
        row_top = jnp.max(scores, axis=-1, keepdims=True)
        expd = jnp.where(allowed, jnp.exp(scores - row_top), 0.0)
        probs = expd / jnp.sum(expd, axis=-1, keepdims=True)
        weights = lax.optimization_barrier(probs.astype(jnp.bfloat16)).astype(jnp.float32)
        attended = jnp.einsum("gqk,gkd->gqd", weights, v_tiles, precision=highest)
        row_delta = jnp.sum(d_group * attended, axis=-1, keepdims=True)
        grad_probs = jnp.einsum("gqd,gkd->gqk", d_group, v_tiles, precision=highest)
        grad_scores = lax.optimization_barrier((probs * (grad_probs - row_delta)).astype(jnp.bfloat16)).astype(jnp.float32)
        query_part = jnp.einsum("gqk,gkd->gqd", grad_scores, k_tiles, precision=highest) * score_scale
        key_part = jnp.einsum("gqk,gqd->gkd", grad_scores, q_group, precision=highest) * score_scale
        value_part = jnp.einsum("gqk,gqd->gkd", weights, d_group, precision=highest)
        flat_index = index_table.reshape(-1)
        key_acc = key_acc.at[flat_index].add(key_part.reshape(groups_now * slot_count, blk_rows, head_dim))
        value_acc = value_acc.at[flat_index].add(value_part.reshape(groups_now * slot_count, blk_rows, head_dim))
        return (key_acc, value_acc), query_part

    zeros_acc = jnp.zeros((nblocks, blk_rows, head_dim), jnp.float32)
    chosen_all = jnp.arange(nblocks, dtype=jnp.int32).reshape(-1, block_group)
    (key_acc, value_acc), query_grad = lax.scan(one_group, (zeros_acc, zeros_acc), chosen_all)
    return query_grad.reshape(nblocks, blk_rows, head_dim), key_acc, value_acc


def reference(queries, key_rows, value_rows, out_grad, vertical, slash_offsets, counts):
    length = queries.shape[0]
    nblocks = length // BLK

    def by_head(matrix):
        return matrix.reshape(nblocks, BLK, HEADS, HEAD_DIM).transpose(2, 0, 1, 3)

    results = lax.map(head_reference, (by_head(queries), by_head(key_rows), by_head(value_rows), by_head(out_grad), vertical, slash_offsets, counts))

    def joined(blocks):
        return blocks.transpose(1, 2, 0, 3).reshape(length, HEADS * HEAD_DIM).astype(jnp.bfloat16)

    return joined(results[0]), joined(results[1]), joined(results[2])
```

```python
import functools

import jax
import jax.numpy as jnp
from jax import lax
from jax.experimental import pallas as pl
from jax.experimental.pallas import tpu as pltpu
from jax.sharding import PartitionSpec as P

HEADS = 16
HEAD_DIM = 128
BLK = 128


block_group = 4


def block_lists(chosen, vert_head, slash_head, count_head, nblocks):
    vert_cap = vert_head.shape[0]
    slash_cap = slash_head.shape[0]
    rows_now = chosen.shape[0]
    vert_index = jnp.broadcast_to(vert_head[None, :], (rows_now, vert_cap))
    vert_valid = jnp.broadcast_to(
        (jnp.arange(vert_cap, dtype=jnp.int32) < count_head[0])[None, :], (rows_now, vert_cap)
    )
    slash_index = chosen[:, None] - slash_head[None, :]
    inside = (slash_index >= 0) & (slash_index < nblocks)
    repeated = jnp.any(
        (vert_index[:, :, None] == slash_index[:, None, :]) & vert_valid[:, :, None], axis=1
    )
    slash_valid = (
        (jnp.arange(slash_cap, dtype=jnp.int32) < count_head[1])[None, :]
        & inside
        & jnp.logical_not(repeated)
    )
    index_table = jnp.clip(jnp.concatenate([vert_index, slash_index], axis=1), 0, nblocks - 1)
    valid_table = jnp.concatenate([vert_valid, slash_valid], axis=1)
    return (index_table, valid_table)


def owner_backward(
    q_blocks, k_blocks, v_blocks, d_blocks, vert_head, slash_head, count_head, chosen_all
):
    nblocks, blk_rows, head_dim = q_blocks.shape
    score_scale = head_dim ** (-0.5)
    vert_cap = vert_head.shape[0]
    trips = count_head[0] + count_head[1]

    def one_group(carried, chosen):
        key_acc, value_acc = carried
        index_table, valid_table = block_lists(chosen, vert_head, slash_head, count_head, nblocks)
        q_group = q_blocks[chosen]
        d_group = d_blocks[chosen]
        group_shape = (chosen.shape[0], blk_rows, 1)

        def fetch(position):
            slot_pick = jnp.where(
                position < count_head[0], position, vert_cap + position - count_head[0]
            )
            column = lax.dynamic_index_in_dim(index_table, slot_pick, 1, keepdims=False)
            usable = lax.dynamic_index_in_dim(valid_table, slot_pick, 1, keepdims=False)[
                :, None, None
            ]
            k_tile = k_blocks[column]
            v_tile = v_blocks[column]
            scores = (
                jnp.einsum("gqd,gkd->gqk", q_group, k_tile, preferred_element_type=jnp.float32)
                * score_scale
            )
            return (column, usable, k_tile, v_tile, scores)

        def row_stats(position, running):
            row_top, row_total = running
            column, usable, k_tile, v_tile, scores = fetch(position)
            new_top = jnp.maximum(
                row_top, jnp.where(usable, jnp.max(scores, axis=-1, keepdims=True), -1e30)
            )
            added = jnp.where(
                usable, jnp.sum(jnp.exp(scores - new_top), axis=-1, keepdims=True), 0.0
            )
            return (new_top, row_total * jnp.exp(row_top - new_top) + added)

        row_top, row_total = lax.fori_loop(
            0,
            trips,
            row_stats,
            (jnp.full(group_shape, -1e30, jnp.float32), jnp.zeros(group_shape, jnp.float32)),
        )

        def probs_of(scores, usable):
            return jnp.where(usable, jnp.exp(scores - row_top) / row_total, 0.0)

        def output_step(position, running):
            column, usable, k_tile, v_tile, scores = fetch(position)
            weights = probs_of(scores, usable).astype(jnp.bfloat16)
            return running + jnp.einsum(
                "gqk,gkd->gqd", weights, v_tile, preferred_element_type=jnp.float32
            )

        attended = lax.fori_loop(
            0, trips, output_step, jnp.zeros((chosen.shape[0], blk_rows, head_dim), jnp.float32)
        )
        row_delta = jnp.sum(d_group.astype(jnp.float32) * attended, axis=-1, keepdims=True)

        def grad_step(position, running):
            query_acc, key_run, value_run = running
            column, usable, k_tile, v_tile, scores = fetch(position)
            probs = probs_of(scores, usable)
            weights = probs.astype(jnp.bfloat16)
            grad_probs = jnp.einsum(
                "gqd,gkd->gqk", d_group, v_tile, preferred_element_type=jnp.float32
            )
            grad_scores = (probs * (grad_probs - row_delta)).astype(jnp.bfloat16)
            query_acc = query_acc + jnp.einsum(
                "gqk,gkd->gqd", grad_scores, k_tile, preferred_element_type=jnp.float32
            )
            key_part = (
                jnp.einsum("gqk,gqd->gkd", grad_scores, q_group, preferred_element_type=jnp.float32)
                * score_scale
            )
            value_part = jnp.einsum(
                "gqk,gqd->gkd", weights, d_group, preferred_element_type=jnp.float32
            )
            return (
                query_acc,
                key_run.at[column].add(key_part),
                value_run.at[column].add(value_part),
            )

        start_query = jnp.zeros((chosen.shape[0], blk_rows, head_dim), jnp.float32)
        query_acc, key_acc, value_acc = lax.fori_loop(
            0, trips, grad_step, (start_query, key_acc, value_acc)
        )
        return ((key_acc, value_acc), query_acc * score_scale)

    zeros_acc = jnp.zeros((nblocks, blk_rows, head_dim), jnp.float32)
    (key_acc, value_acc), query_grad = lax.scan(one_group, (zeros_acc, zeros_acc), chosen_all)
    return (query_grad.reshape(-1, blk_rows, head_dim), key_acc, value_acc)


def split_head_body(queries, key_rows, value_rows, out_grad, vertical, slash_offsets, counts):
    tokens_here = queries.shape[0]
    device_count = lax.axis_size("seq")
    device_here = lax.axis_index("seq")
    full_width = HEADS * HEAD_DIM

    def doubled(matrix):
        return jnp.repeat(matrix.reshape(tokens_here, HEADS, HEAD_DIM), 2, axis=1)

    q_owned, k_owned, v_owned, d_owned = (
        lax.all_to_all(doubled(queries), "seq", split_axis=1, concat_axis=0, tiled=True),
        lax.all_to_all(doubled(key_rows), "seq", split_axis=1, concat_axis=0, tiled=True),
        lax.all_to_all(doubled(value_rows), "seq", split_axis=1, concat_axis=0, tiled=True),
        lax.all_to_all(doubled(out_grad), "seq", split_axis=1, concat_axis=0, tiled=True),
    )
    length = tokens_here * device_count
    nblocks = length // BLK
    per_device = 2 * HEADS // device_count
    query_parts = []
    key_parts = []
    value_parts = []
    for local_slot in range(per_device):
        slot_index = device_here * per_device + local_slot
        head_index = slot_index // 2
        parity = slot_index % 2
        chosen_all = (parity + 2 * jnp.arange(nblocks // 2, dtype=jnp.int32)).reshape(
            -1, block_group
        )

        def blockwise(matrix):
            return matrix[:, local_slot, :].reshape(nblocks, BLK, HEAD_DIM)

        query_sel, key_acc, value_acc = owner_backward(
            blockwise(q_owned),
            blockwise(k_owned),
            blockwise(v_owned),
            blockwise(d_owned),
            vertical[head_index],
            slash_offsets[head_index],
            counts[head_index],
            chosen_all,
        )
        query_full = (
            jnp.zeros((nblocks, BLK, HEAD_DIM), jnp.float32)
            .at[chosen_all.reshape(-1)]
            .set(query_sel)
        )
        query_parts.append(query_full.reshape(length, HEAD_DIM))
        key_parts.append(key_acc.reshape(length, HEAD_DIM))
        value_parts.append(value_acc.reshape(length, HEAD_DIM))
    all_parts = (query_parts, key_parts, value_parts)
    stacked = [jnp.stack(member, axis=1) for member in all_parts]
    returned = (
        lax.all_to_all(stacked[0], "seq", split_axis=0, concat_axis=1, tiled=True),
        lax.all_to_all(stacked[1], "seq", split_axis=0, concat_axis=1, tiled=True),
        lax.all_to_all(stacked[2], "seq", split_axis=0, concat_axis=1, tiled=True),
    )
    results = [
        back.reshape(tokens_here, HEADS, 2, HEAD_DIM)
        .sum(axis=2)
        .astype(jnp.bfloat16)
        .reshape(tokens_here, full_width)
        for back in returned
    ]
    return (results[0], results[1], results[2])


MESH = pl.DeviceIdType.MESH
QUERY_TILE = 256
LOG2E = 1.4426950408889634
NEVER = -1e30


def fused_kernel(
    count,
    per_device,
    k_in,
    v_in,
    q_in,
    d_in,
    vertical,
    slash_offsets,
    counts,
    dq_out,
    dk_out,
    dv_out,
    arrived,
    finished,
    bias,
    key_acc,
    value_acc,
    fwd_send,
    fwd_recv,
    fwd_local,
    back_send,
    back_recv,
    back_local,
):
    me = lax.axis_index("seq")
    sources = (k_in, v_in, q_in, d_in)
    targets = (dk_out, dv_out, dq_out)
    length = count * BLK
    score_scale = HEAD_DIM ** (-0.5)

    def offset_of(step):
        return count // 2 + ((step + 1) // 2) * (2 * (step % 2) - 1)

    def rows_of(index):
        return pl.ds(pl.multiple_of(index * BLK, BLK), BLK)

    def columns_of(owner, slot):
        return pl.ds(pl.multiple_of((owner * per_device + slot) * HEAD_DIM, HEAD_DIM), HEAD_DIM)

    def forward(which, slot, step, sending):
        peer = lax.rem(me + offset_of(step), count)
        source = lax.rem(me + count - offset_of(step), count)
        return pltpu.make_async_remote_copy(
            src_ref=sources[which].at[:, columns_of(peer, slot)],
            dst_ref=arrived.at[which, slot, rows_of(me if sending else source), :],
            send_sem=fwd_send.at[which, slot, step],
            recv_sem=fwd_recv.at[which, slot, step],
            device_id={"seq": peer},
            device_id_type=MESH,
        )

    def own_forward(which, slot):
        return pltpu.make_async_copy(
            sources[which].at[:, columns_of(me, slot)],
            arrived.at[which, slot, rows_of(me), :],
            fwd_local.at[which, slot],
        )

    def backward(which, slot, step, sending):
        peer = lax.rem(me + offset_of(step), count)
        source = lax.rem(me + count - offset_of(step), count)
        return pltpu.make_async_remote_copy(
            src_ref=finished.at[which, slot, rows_of(peer), :],
            dst_ref=targets[which].at[:, columns_of(me if sending else source, slot)],
            send_sem=back_send.at[which, slot, step],
            recv_sem=back_recv.at[which, slot, step],
            device_id={"seq": peer},
            device_id_type=MESH,
        )

    def own_backward(which, slot):
        return pltpu.make_async_copy(
            finished.at[which, slot, rows_of(me), :],
            targets[which].at[:, columns_of(me, slot)],
            back_local.at[which, slot],
        )

    def each_step(do):
        @pl.loop(0, count - 1)
        def _(step):
            do(step)

    barrier = pltpu.get_barrier_semaphore()

    @pl.loop(1, count)
    def _(step):
        pl.semaphore_signal(
            barrier, inc=1, device_id={"seq": lax.rem(me + step, count)}, device_id_type=MESH
        )

    pl.semaphore_wait(barrier, count - 1)

    for slot in range(per_device):

        def send_all(step, slot=slot):
            for which in range(4):
                forward(which, slot, step, True).start()

        each_step(send_all)
        for which in range(4):
            own_forward(which, slot).start()

    query_block = lax.broadcasted_iota(jnp.int32, (count, length), 0)
    key_block = lax.broadcasted_iota(jnp.int32, (count, length), 1) // BLK
    for slot in range(per_device):
        head = me * per_device + slot
        allowed = jnp.zeros((count, length), jnp.float32)
        for entry in range(vertical.shape[1]):
            wanted = jnp.where(entry < counts[head, 0], vertical[head, entry], -1)
            allowed = jnp.where(key_block == wanted, 1.0, allowed)
        for entry in range(slash_offsets.shape[1]):
            wanted = jnp.where(entry < counts[head, 1], slash_offsets[head, entry], 2 * count)
            allowed = jnp.where(query_block - key_block == wanted, 1.0, allowed)
        bias[slot] = jnp.where(allowed > 0.0, 0.0, NEVER)

    def dot(a, b, a_dim, b_dim):
        return lax.dot_general(
            a, b, (((a_dim,), (b_dim,)), ((), ())), preferred_element_type=jnp.float32
        )

    for slot in range(per_device):

        def arrive(step, slot=slot):
            for which in range(4):
                forward(which, slot, step, False).wait_recv()

        each_step(arrive)
        for which in range(4):
            own_forward(which, slot).wait()

        key_acc[...] = jnp.zeros_like(key_acc)
        value_acc[...] = jnp.zeros_like(value_acc)

        @pl.loop(0, length // QUERY_TILE)
        def _(tile, slot=slot):
            rows = pl.ds(pl.multiple_of(tile * QUERY_TILE, QUERY_TILE), QUERY_TILE)
            keys = arrived[0, slot]
            values = arrived[1, slot]
            q_tile = arrived[2, slot, rows, :]
            d_tile = arrived[3, slot, rows, :]
            blocks_here = QUERY_TILE // BLK
            mask = jnp.concatenate(
                [
                    jnp.broadcast_to(
                        bias[slot, pl.ds(tile * blocks_here + part, 1), :], (BLK, length)
                    )
                    for part in range(blocks_here)
                ],
                axis=0,
            )
            scores = dot(q_tile, keys, 1, 1) * (score_scale * LOG2E) + mask
            top = jnp.max(scores, axis=-1, keepdims=True)
            raised = jnp.exp2(scores - top)
            total = jnp.sum(raised, axis=-1, keepdims=True)
            probs = raised * (1.0 / total)
            weights = probs.astype(jnp.bfloat16)
            attended = dot(weights, values, 1, 0)
            row_delta = jnp.sum(d_tile.astype(jnp.float32) * attended, axis=-1, keepdims=True)
            grad_probs = dot(d_tile, values, 1, 1)
            grad_scores = (probs * (grad_probs - row_delta)).astype(jnp.bfloat16)
            finished[2, slot, rows, :] = (dot(grad_scores, keys, 1, 0) * score_scale).astype(
                jnp.bfloat16
            )
            key_acc[...] += dot(q_tile, grad_scores, 0, 0)
            value_acc[...] += dot(d_tile, weights, 0, 0)

        finished[0, slot] = (key_acc[...] * score_scale).T.astype(jnp.bfloat16)
        finished[1, slot] = value_acc[...].T.astype(jnp.bfloat16)

        def give_back(step, slot=slot):
            for which in range(3):
                backward(which, slot, step, True).start()

        each_step(give_back)
        for which in range(3):
            own_backward(which, slot).start()

    for slot in range(per_device):

        def drain(step, slot=slot):
            for which in range(4):
                forward(which, slot, step, True).wait_send()
            for which in range(3):
                backward(which, slot, step, True).wait_send()
                backward(which, slot, step, False).wait_recv()

        each_step(drain)
        for which in range(3):
            own_backward(which, slot).wait()


def whole_head_body(queries, key_rows, value_rows, out_grad, vertical, slash_offsets, counts):
    count = lax.axis_size("seq")
    per_device = HEADS // count
    length = count * BLK
    anywhere = pl.BlockSpec(memory_space=pl.ANY)
    scalars = pl.BlockSpec(memory_space=pltpu.SMEM)
    shape = jax.ShapeDtypeStruct(queries.shape, queries.dtype)
    sems = pltpu.SemaphoreType.DMA
    return pl.pallas_call(
        functools.partial(fused_kernel, count, per_device),
        out_shape=(shape, shape, shape),
        in_specs=[anywhere] * 4 + [scalars] * 3,
        out_specs=(anywhere, anywhere, anywhere),
        scratch_shapes=[
            pltpu.VMEM((4, per_device, length, HEAD_DIM), jnp.bfloat16),
            pltpu.VMEM((3, per_device, length, HEAD_DIM), jnp.bfloat16),
            pltpu.VMEM((per_device, count, length), jnp.float32),
            pltpu.VMEM((HEAD_DIM, length), jnp.float32),
            pltpu.VMEM((HEAD_DIM, length), jnp.float32),
            sems((4, per_device, count - 1)),
            sems((4, per_device, count - 1)),
            sems((4, per_device)),
            sems((3, per_device, count - 1)),
            sems((3, per_device, count - 1)),
            sems((3, per_device)),
        ],
        compiler_params=pltpu.CompilerParams(
            collective_id=0, has_side_effects=True, vmem_limit_bytes=40 * 1024 * 1024
        ),
    )(key_rows, value_rows, queries, out_grad, vertical, slash_offsets, counts)


def solution(mesh):
    whole_heads = HEADS % mesh.shape["seq"] == 0
    return jax.shard_map(
        whole_head_body if whole_heads else split_head_body,
        mesh=mesh,
        in_specs=(
            P(("doc", "seq"), None),
            P(("doc", "seq"), None),
            P(("doc", "seq"), None),
            P(("doc", "seq"), None),
            P("doc", None),
            P("doc", None),
            P("doc", None),
        ),
        out_specs=(P(("doc", "seq"), None), P(("doc", "seq"), None), P(("doc", "seq"), None)),
        check_vma=False,
    )
```

```python
import functools

import jax
import jax.numpy as jnp
from jax import lax
from jax.experimental import pallas as pl
from jax.experimental.pallas import tpu as pltpu
from jax.sharding import PartitionSpec as P

HEADS = 16
HEAD_DIM = 128
BLK = 128


block_group = 4


def block_lists(chosen, vert_head, slash_head, count_head, nblocks):
    vert_cap = vert_head.shape[0]
    slash_cap = slash_head.shape[0]
    rows_now = chosen.shape[0]
    vert_index = jnp.broadcast_to(vert_head[None, :], (rows_now, vert_cap))
    vert_valid = jnp.broadcast_to(
        (jnp.arange(vert_cap, dtype=jnp.int32) < count_head[0])[None, :], (rows_now, vert_cap)
    )
    slash_index = chosen[:, None] - slash_head[None, :]
    inside = (slash_index >= 0) & (slash_index < nblocks)
    repeated = jnp.any(
        (vert_index[:, :, None] == slash_index[:, None, :]) & vert_valid[:, :, None], axis=1
    )
    slash_valid = (
        (jnp.arange(slash_cap, dtype=jnp.int32) < count_head[1])[None, :]
        & inside
        & jnp.logical_not(repeated)
    )
    index_table = jnp.clip(jnp.concatenate([vert_index, slash_index], axis=1), 0, nblocks - 1)
    valid_table = jnp.concatenate([vert_valid, slash_valid], axis=1)
    return (index_table, valid_table)


def owner_backward(
    q_blocks, k_blocks, v_blocks, d_blocks, vert_head, slash_head, count_head, chosen_all
):
    nblocks, blk_rows, head_dim = q_blocks.shape
    score_scale = head_dim ** (-0.5)
    vert_cap = vert_head.shape[0]
    trips = count_head[0] + count_head[1]

    def one_group(carried, chosen):
        key_acc, value_acc = carried
        index_table, valid_table = block_lists(chosen, vert_head, slash_head, count_head, nblocks)
        q_group = q_blocks[chosen]
        d_group = d_blocks[chosen]
        group_shape = (chosen.shape[0], blk_rows, 1)

        def fetch(position):
            slot_pick = jnp.where(
                position < count_head[0], position, vert_cap + position - count_head[0]
            )
            column = lax.dynamic_index_in_dim(index_table, slot_pick, 1, keepdims=False)
            usable = lax.dynamic_index_in_dim(valid_table, slot_pick, 1, keepdims=False)[
                :, None, None
            ]
            k_tile = k_blocks[column]
            v_tile = v_blocks[column]
            scores = (
                jnp.einsum("gqd,gkd->gqk", q_group, k_tile, preferred_element_type=jnp.float32)
                * score_scale
            )
            return (column, usable, k_tile, v_tile, scores)

        def row_stats(position, running):
            row_top, row_total = running
            column, usable, k_tile, v_tile, scores = fetch(position)
            new_top = jnp.maximum(
                row_top, jnp.where(usable, jnp.max(scores, axis=-1, keepdims=True), -1e30)
            )
            added = jnp.where(
                usable, jnp.sum(jnp.exp(scores - new_top), axis=-1, keepdims=True), 0.0
            )
            return (new_top, row_total * jnp.exp(row_top - new_top) + added)

        row_top, row_total = lax.fori_loop(
            0,
            trips,
            row_stats,
            (jnp.full(group_shape, -1e30, jnp.float32), jnp.zeros(group_shape, jnp.float32)),
        )

        def probs_of(scores, usable):
            return jnp.where(usable, jnp.exp(scores - row_top) / row_total, 0.0)

        def output_step(position, running):
            column, usable, k_tile, v_tile, scores = fetch(position)
            weights = probs_of(scores, usable).astype(jnp.bfloat16)
            return running + jnp.einsum(
                "gqk,gkd->gqd", weights, v_tile, preferred_element_type=jnp.float32
            )

        attended = lax.fori_loop(
            0, trips, output_step, jnp.zeros((chosen.shape[0], blk_rows, head_dim), jnp.float32)
        )
        row_delta = jnp.sum(d_group.astype(jnp.float32) * attended, axis=-1, keepdims=True)

        def grad_step(position, running):
            query_acc, key_run, value_run = running
            column, usable, k_tile, v_tile, scores = fetch(position)
            probs = probs_of(scores, usable)
            weights = probs.astype(jnp.bfloat16)
            grad_probs = jnp.einsum(
                "gqd,gkd->gqk", d_group, v_tile, preferred_element_type=jnp.float32
            )
            grad_scores = (probs * (grad_probs - row_delta)).astype(jnp.bfloat16)
            query_acc = query_acc + jnp.einsum(
                "gqk,gkd->gqd", grad_scores, k_tile, preferred_element_type=jnp.float32
            )
            key_part = (
                jnp.einsum("gqk,gqd->gkd", grad_scores, q_group, preferred_element_type=jnp.float32)
                * score_scale
            )
            value_part = jnp.einsum(
                "gqk,gqd->gkd", weights, d_group, preferred_element_type=jnp.float32
            )
            return (
                query_acc,
                key_run.at[column].add(key_part),
                value_run.at[column].add(value_part),
            )

        start_query = jnp.zeros((chosen.shape[0], blk_rows, head_dim), jnp.float32)
        query_acc, key_acc, value_acc = lax.fori_loop(
            0, trips, grad_step, (start_query, key_acc, value_acc)
        )
        return ((key_acc, value_acc), query_acc * score_scale)

    zeros_acc = jnp.zeros((nblocks, blk_rows, head_dim), jnp.float32)
    (key_acc, value_acc), query_grad = lax.scan(one_group, (zeros_acc, zeros_acc), chosen_all)
    return (query_grad.reshape(-1, blk_rows, head_dim), key_acc, value_acc)


def split_head_body(queries, key_rows, value_rows, out_grad, vertical, slash_offsets, counts):
    tokens_here = queries.shape[0]
    device_count = lax.axis_size("seq")
    device_here = lax.axis_index("seq")
    full_width = HEADS * HEAD_DIM

    def doubled(matrix):
        return jnp.repeat(matrix.reshape(tokens_here, HEADS, HEAD_DIM), 2, axis=1)

    q_owned, k_owned, v_owned, d_owned = (
        lax.all_to_all(doubled(queries), "seq", split_axis=1, concat_axis=0, tiled=True),
        lax.all_to_all(doubled(key_rows), "seq", split_axis=1, concat_axis=0, tiled=True),
        lax.all_to_all(doubled(value_rows), "seq", split_axis=1, concat_axis=0, tiled=True),
        lax.all_to_all(doubled(out_grad), "seq", split_axis=1, concat_axis=0, tiled=True),
    )
    length = tokens_here * device_count
    nblocks = length // BLK
    per_device = 2 * HEADS // device_count
    query_parts = []
    key_parts = []
    value_parts = []
    for local_slot in range(per_device):
        slot_index = device_here * per_device + local_slot
        head_index = slot_index // 2
        parity = slot_index % 2
        chosen_all = (parity + 2 * jnp.arange(nblocks // 2, dtype=jnp.int32)).reshape(
            -1, block_group
        )

        def blockwise(matrix):
            return matrix[:, local_slot, :].reshape(nblocks, BLK, HEAD_DIM)

        query_sel, key_acc, value_acc = owner_backward(
            blockwise(q_owned),
            blockwise(k_owned),
            blockwise(v_owned),
            blockwise(d_owned),
            vertical[head_index],
            slash_offsets[head_index],
            counts[head_index],
            chosen_all,
        )
        query_full = (
            jnp.zeros((nblocks, BLK, HEAD_DIM), jnp.float32)
            .at[chosen_all.reshape(-1)]
            .set(query_sel)
        )
        query_parts.append(query_full.reshape(length, HEAD_DIM))
        key_parts.append(key_acc.reshape(length, HEAD_DIM))
        value_parts.append(value_acc.reshape(length, HEAD_DIM))
    all_parts = (query_parts, key_parts, value_parts)
    stacked = [jnp.stack(member, axis=1) for member in all_parts]
    returned = (
        lax.all_to_all(stacked[0], "seq", split_axis=0, concat_axis=1, tiled=True),
        lax.all_to_all(stacked[1], "seq", split_axis=0, concat_axis=1, tiled=True),
        lax.all_to_all(stacked[2], "seq", split_axis=0, concat_axis=1, tiled=True),
    )
    results = [
        back.reshape(tokens_here, HEADS, 2, HEAD_DIM)
        .sum(axis=2)
        .astype(jnp.bfloat16)
        .reshape(tokens_here, full_width)
        for back in returned
    ]
    return (results[0], results[1], results[2])


MESH = pl.DeviceIdType.MESH
QUERY_TILE = 256
LOG2E = 1.4426950408889634
NEVER = -1e30


def fused_kernel(
    count,
    per_device,
    k_in,
    v_in,
    q_in,
    d_in,
    vertical,
    slash_offsets,
    counts,
    dq_out,
    dk_out,
    dv_out,
    arrived,
    finished,
    bias,
    key_acc,
    value_acc,
    fwd_send,
    fwd_recv,
    fwd_local,
    back_send,
    back_recv,
    back_local,
):
    me = lax.axis_index("seq")
    sources = (k_in, v_in, q_in, d_in)
    targets = (dk_out, dv_out, dq_out)
    length = count * BLK
    score_scale = HEAD_DIM ** (-0.5)

    def offset_of(step):
        return count // 2 + ((step + 1) // 2) * (2 * (step % 2) - 1)

    def rows_of(index):
        return pl.ds(pl.multiple_of(index * BLK, BLK), BLK)

    def columns_of(owner, slot):
        return pl.ds(pl.multiple_of((owner * per_device + slot) * HEAD_DIM, HEAD_DIM), HEAD_DIM)

    def forward(which, slot, step, sending):
        peer = lax.rem(me + offset_of(step), count)
        source = lax.rem(me + count - offset_of(step), count)
        return pltpu.make_async_remote_copy(
            src_ref=sources[which].at[:, columns_of(peer, slot)],
            dst_ref=arrived.at[which, slot, rows_of(me if sending else source), :],
            send_sem=fwd_send.at[which, slot, step],
            recv_sem=fwd_recv.at[which, slot, step],
            device_id={"seq": peer},
            device_id_type=MESH,
        )

    def own_forward(which, slot):
        return pltpu.make_async_copy(
            sources[which].at[:, columns_of(me, slot)],
            arrived.at[which, slot, rows_of(me), :],
            fwd_local.at[which, slot],
        )

    def backward(which, slot, step, sending):
        peer = lax.rem(me + offset_of(step), count)
        source = lax.rem(me + count - offset_of(step), count)
        return pltpu.make_async_remote_copy(
            src_ref=finished.at[which, slot, rows_of(peer), :],
            dst_ref=targets[which].at[:, columns_of(me if sending else source, slot)],
            send_sem=back_send.at[which, slot, step],
            recv_sem=back_recv.at[which, slot, step],
            device_id={"seq": peer},
            device_id_type=MESH,
        )

    def own_backward(which, slot):
        return pltpu.make_async_copy(
            finished.at[which, slot, rows_of(me), :],
            targets[which].at[:, columns_of(me, slot)],
            back_local.at[which, slot],
        )

    def each_step(do):
        @pl.loop(0, count - 1)
        def _(step):
            do(step)

    barrier = pltpu.get_barrier_semaphore()

    @pl.loop(1, count)
    def _(step):
        pl.semaphore_signal(
            barrier, inc=1, device_id={"seq": lax.rem(me + step, count)}, device_id_type=MESH
        )

    pl.semaphore_wait(barrier, count - 1)

    for slot in range(per_device):

        def send_all(step, slot=slot):
            for which in range(4):
                forward(which, slot, step, True).start()

        each_step(send_all)
        for which in range(4):
            own_forward(which, slot).start()

    query_block = lax.broadcasted_iota(jnp.int32, (count, length), 0)
    key_block = lax.broadcasted_iota(jnp.int32, (count, length), 1) // BLK
    for slot in range(per_device):
        head = me * per_device + slot
        allowed = jnp.zeros((count, length), jnp.float32)
        for entry in range(vertical.shape[0]):
            wanted = jnp.where(entry < counts[0, head], vertical[entry, head], -1)
            allowed = jnp.where(key_block == wanted, 1.0, allowed)
        for entry in range(slash_offsets.shape[0]):
            wanted = jnp.where(entry < counts[1, head], slash_offsets[entry, head], 2 * count)
            allowed = jnp.where(query_block - key_block == wanted, 1.0, allowed)
        bias[slot] = jnp.where(allowed > 0.0, 0.0, NEVER)

    def dot(a, b, a_dim, b_dim):
        return lax.dot_general(
            a, b, (((a_dim,), (b_dim,)), ((), ())), preferred_element_type=jnp.float32
        )

    for slot in range(per_device):

        def arrive(step, slot=slot):
            for which in range(4):
                forward(which, slot, step, False).wait_recv()

        each_step(arrive)
        for which in range(4):
            own_forward(which, slot).wait()

        key_acc[...] = jnp.zeros_like(key_acc)
        value_acc[...] = jnp.zeros_like(value_acc)

        @pl.loop(0, length // QUERY_TILE)
        def _(tile, slot=slot):
            rows = pl.ds(pl.multiple_of(tile * QUERY_TILE, QUERY_TILE), QUERY_TILE)
            keys = arrived[0, slot]
            values = arrived[1, slot]
            q_tile = arrived[2, slot, rows, :]
            d_tile = arrived[3, slot, rows, :]
            blocks_here = QUERY_TILE // BLK
            mask = jnp.concatenate(
                [
                    jnp.broadcast_to(
                        bias[slot, pl.ds(tile * blocks_here + part, 1), :], (BLK, length)
                    )
                    for part in range(blocks_here)
                ],
                axis=0,
            )
            scores = dot(q_tile, keys, 1, 1) * (score_scale * LOG2E) + mask
            top = jnp.max(scores, axis=-1, keepdims=True)
            raised = jnp.exp2(scores - top)
            total = jnp.sum(raised, axis=-1, keepdims=True)
            probs = raised * (1.0 / total)
            weights = probs.astype(jnp.bfloat16)
            attended = dot(weights, values, 1, 0)
            row_delta = jnp.sum(d_tile.astype(jnp.float32) * attended, axis=-1, keepdims=True)
            grad_probs = dot(d_tile, values, 1, 1)
            grad_scores = (probs * (grad_probs - row_delta)).astype(jnp.bfloat16)
            finished[2, slot, rows, :] = (dot(grad_scores, keys, 1, 0) * score_scale).astype(
                jnp.bfloat16
            )
            key_acc[...] += dot(q_tile, grad_scores, 0, 0)
            value_acc[...] += dot(d_tile, weights, 0, 0)

        finished[0, slot] = (key_acc[...] * score_scale).T.astype(jnp.bfloat16)
        finished[1, slot] = value_acc[...].T.astype(jnp.bfloat16)

        def give_back(step, slot=slot):
            for which in range(3):
                backward(which, slot, step, True).start()

        each_step(give_back)
        for which in range(3):
            own_backward(which, slot).start()

    for slot in range(per_device):

        def drain(step, slot=slot):
            for which in range(4):
                forward(which, slot, step, True).wait_send()
            for which in range(3):
                backward(which, slot, step, True).wait_send()
                backward(which, slot, step, False).wait_recv()

        each_step(drain)
        for which in range(3):
            own_backward(which, slot).wait()


def store_kernel(dq_in, dk_in, dv_in, dq_out, dk_out, dv_out, done):
    pairs = ((dq_in, dq_out), (dk_in, dk_out), (dv_in, dv_out))
    copies = [pltpu.make_async_copy(a, b, done.at[i]) for i, (a, b) in enumerate(pairs)]
    for copy in copies:
        copy.start()
    for copy in copies:
        copy.wait()


def whole_head_body(queries, key_rows, value_rows, out_grad, vertical, slash_offsets, counts):
    count = lax.axis_size("seq")
    per_device = HEADS // count
    length = count * BLK
    anywhere = pl.BlockSpec(memory_space=pl.ANY)
    scalars = pl.BlockSpec(memory_space=pltpu.SMEM)
    shape = jax.ShapeDtypeStruct(queries.shape, queries.dtype)
    sems = pltpu.SemaphoreType.DMA
    query_grad, key_grad, value_grad = pl.pallas_call(
        functools.partial(fused_kernel, count, per_device),
        out_shape=(shape, shape, shape),
        in_specs=[anywhere] * 4 + [scalars] * 3,
        out_specs=(anywhere, anywhere, anywhere),
        scratch_shapes=[
            pltpu.VMEM((4, per_device, length, HEAD_DIM), jnp.bfloat16),
            pltpu.VMEM((3, per_device, length, HEAD_DIM), jnp.bfloat16),
            pltpu.VMEM((per_device, count, length), jnp.float32),
            pltpu.VMEM((HEAD_DIM, length), jnp.float32),
            pltpu.VMEM((HEAD_DIM, length), jnp.float32),
            sems((4, per_device, count - 1)),
            sems((4, per_device, count - 1)),
            sems((4, per_device)),
            sems((3, per_device, count - 1)),
            sems((3, per_device, count - 1)),
            sems((3, per_device)),
        ],
        compiler_params=pltpu.CompilerParams(
            collective_id=0, has_side_effects=True, vmem_limit_bytes=64 * 1024 * 1024
        ),
    )(key_rows, value_rows, queries, out_grad, vertical.T, slash_offsets.T, counts.T)
    return pl.pallas_call(
        store_kernel,
        out_shape=(shape, shape, shape),
        in_specs=[anywhere] * 3,
        out_specs=(anywhere,) * 3,
        scratch_shapes=[sems((3,))],
        compiler_params=pltpu.CompilerParams(vmem_limit_bytes=64 * 1024 * 1024),
    )(query_grad, key_grad, value_grad)


def solution(mesh):
    whole_heads = HEADS % mesh.shape["seq"] == 0
    return jax.shard_map(
        whole_head_body if whole_heads else split_head_body,
        mesh=mesh,
        in_specs=(
            P(("doc", "seq"), None),
            P(("doc", "seq"), None),
            P(("doc", "seq"), None),
            P(("doc", "seq"), None),
            P("doc", None),
            P("doc", None),
            P("doc", None),
        ),
        out_specs=(P(("doc", "seq"), None), P(("doc", "seq"), None), P(("doc", "seq"), None)),
        check_vma=False,
    )
```

```python
import functools

import jax
import jax.numpy as jnp
from jax import lax
from jax.experimental import pallas as pl
from jax.experimental.pallas import tpu as pltpu
from jax.sharding import PartitionSpec as P

HEADS = 16
HEAD_DIM = 128
BLK = 128


block_group = 4


def block_lists(chosen, vert_head, slash_head, count_head, nblocks):
    vert_cap = vert_head.shape[0]
    slash_cap = slash_head.shape[0]
    rows_now = chosen.shape[0]
    vert_index = jnp.broadcast_to(vert_head[None, :], (rows_now, vert_cap))
    vert_valid = jnp.broadcast_to(
        (jnp.arange(vert_cap, dtype=jnp.int32) < count_head[0])[None, :], (rows_now, vert_cap)
    )
    slash_index = chosen[:, None] - slash_head[None, :]
    inside = (slash_index >= 0) & (slash_index < nblocks)
    repeated = jnp.any(
        (vert_index[:, :, None] == slash_index[:, None, :]) & vert_valid[:, :, None], axis=1
    )
    slash_valid = (
        (jnp.arange(slash_cap, dtype=jnp.int32) < count_head[1])[None, :]
        & inside
        & jnp.logical_not(repeated)
    )
    index_table = jnp.clip(jnp.concatenate([vert_index, slash_index], axis=1), 0, nblocks - 1)
    valid_table = jnp.concatenate([vert_valid, slash_valid], axis=1)
    return (index_table, valid_table)


def owner_backward(
    q_blocks, k_blocks, v_blocks, d_blocks, vert_head, slash_head, count_head, chosen_all
):
    nblocks, blk_rows, head_dim = q_blocks.shape
    score_scale = head_dim ** (-0.5)
    vert_cap = vert_head.shape[0]
    trips = count_head[0] + count_head[1]

    def one_group(carried, chosen):
        key_acc, value_acc = carried
        index_table, valid_table = block_lists(chosen, vert_head, slash_head, count_head, nblocks)
        q_group = q_blocks[chosen]
        d_group = d_blocks[chosen]
        group_shape = (chosen.shape[0], blk_rows, 1)

        def fetch(position):
            slot_pick = jnp.where(
                position < count_head[0], position, vert_cap + position - count_head[0]
            )
            column = lax.dynamic_index_in_dim(index_table, slot_pick, 1, keepdims=False)
            usable = lax.dynamic_index_in_dim(valid_table, slot_pick, 1, keepdims=False)[
                :, None, None
            ]
            k_tile = k_blocks[column]
            v_tile = v_blocks[column]
            scores = (
                jnp.einsum("gqd,gkd->gqk", q_group, k_tile, preferred_element_type=jnp.float32)
                * score_scale
            )
            return (column, usable, k_tile, v_tile, scores)

        def row_stats(position, running):
            row_top, row_total = running
            column, usable, k_tile, v_tile, scores = fetch(position)
            new_top = jnp.maximum(
                row_top, jnp.where(usable, jnp.max(scores, axis=-1, keepdims=True), -1e30)
            )
            added = jnp.where(
                usable, jnp.sum(jnp.exp(scores - new_top), axis=-1, keepdims=True), 0.0
            )
            return (new_top, row_total * jnp.exp(row_top - new_top) + added)

        row_top, row_total = lax.fori_loop(
            0,
            trips,
            row_stats,
            (jnp.full(group_shape, -1e30, jnp.float32), jnp.zeros(group_shape, jnp.float32)),
        )

        def probs_of(scores, usable):
            return jnp.where(usable, jnp.exp(scores - row_top) / row_total, 0.0)

        def output_step(position, running):
            column, usable, k_tile, v_tile, scores = fetch(position)
            weights = probs_of(scores, usable).astype(jnp.bfloat16)
            return running + jnp.einsum(
                "gqk,gkd->gqd", weights, v_tile, preferred_element_type=jnp.float32
            )

        attended = lax.fori_loop(
            0, trips, output_step, jnp.zeros((chosen.shape[0], blk_rows, head_dim), jnp.float32)
        )
        row_delta = jnp.sum(d_group.astype(jnp.float32) * attended, axis=-1, keepdims=True)

        def grad_step(position, running):
            query_acc, key_run, value_run = running
            column, usable, k_tile, v_tile, scores = fetch(position)
            probs = probs_of(scores, usable)
            weights = probs.astype(jnp.bfloat16)
            grad_probs = jnp.einsum(
                "gqd,gkd->gqk", d_group, v_tile, preferred_element_type=jnp.float32
            )
            grad_scores = (probs * (grad_probs - row_delta)).astype(jnp.bfloat16)
            query_acc = query_acc + jnp.einsum(
                "gqk,gkd->gqd", grad_scores, k_tile, preferred_element_type=jnp.float32
            )
            key_part = (
                jnp.einsum("gqk,gqd->gkd", grad_scores, q_group, preferred_element_type=jnp.float32)
                * score_scale
            )
            value_part = jnp.einsum(
                "gqk,gqd->gkd", weights, d_group, preferred_element_type=jnp.float32
            )
            return (
                query_acc,
                key_run.at[column].add(key_part),
                value_run.at[column].add(value_part),
            )

        start_query = jnp.zeros((chosen.shape[0], blk_rows, head_dim), jnp.float32)
        query_acc, key_acc, value_acc = lax.fori_loop(
            0, trips, grad_step, (start_query, key_acc, value_acc)
        )
        return ((key_acc, value_acc), query_acc * score_scale)

    zeros_acc = jnp.zeros((nblocks, blk_rows, head_dim), jnp.float32)
    (key_acc, value_acc), query_grad = lax.scan(one_group, (zeros_acc, zeros_acc), chosen_all)
    return (query_grad.reshape(-1, blk_rows, head_dim), key_acc, value_acc)


def split_head_body(queries, key_rows, value_rows, out_grad, vertical, slash_offsets, counts):
    tokens_here = queries.shape[0]
    device_count = lax.axis_size("seq")
    device_here = lax.axis_index("seq")
    full_width = HEADS * HEAD_DIM

    def doubled(matrix):
        return jnp.repeat(matrix.reshape(tokens_here, HEADS, HEAD_DIM), 2, axis=1)

    q_owned, k_owned, v_owned, d_owned = (
        lax.all_to_all(doubled(queries), "seq", split_axis=1, concat_axis=0, tiled=True),
        lax.all_to_all(doubled(key_rows), "seq", split_axis=1, concat_axis=0, tiled=True),
        lax.all_to_all(doubled(value_rows), "seq", split_axis=1, concat_axis=0, tiled=True),
        lax.all_to_all(doubled(out_grad), "seq", split_axis=1, concat_axis=0, tiled=True),
    )
    length = tokens_here * device_count
    nblocks = length // BLK
    per_device = 2 * HEADS // device_count
    query_parts = []
    key_parts = []
    value_parts = []
    for local_slot in range(per_device):
        slot_index = device_here * per_device + local_slot
        head_index = slot_index // 2
        parity = slot_index % 2
        chosen_all = (parity + 2 * jnp.arange(nblocks // 2, dtype=jnp.int32)).reshape(
            -1, block_group
        )

        def blockwise(matrix):
            return matrix[:, local_slot, :].reshape(nblocks, BLK, HEAD_DIM)

        query_sel, key_acc, value_acc = owner_backward(
            blockwise(q_owned),
            blockwise(k_owned),
            blockwise(v_owned),
            blockwise(d_owned),
            vertical[head_index],
            slash_offsets[head_index],
            counts[head_index],
            chosen_all,
        )
        query_full = (
            jnp.zeros((nblocks, BLK, HEAD_DIM), jnp.float32)
            .at[chosen_all.reshape(-1)]
            .set(query_sel)
        )
        query_parts.append(query_full.reshape(length, HEAD_DIM))
        key_parts.append(key_acc.reshape(length, HEAD_DIM))
        value_parts.append(value_acc.reshape(length, HEAD_DIM))
    all_parts = (query_parts, key_parts, value_parts)
    stacked = [jnp.stack(member, axis=1) for member in all_parts]
    returned = (
        lax.all_to_all(stacked[0], "seq", split_axis=0, concat_axis=1, tiled=True),
        lax.all_to_all(stacked[1], "seq", split_axis=0, concat_axis=1, tiled=True),
        lax.all_to_all(stacked[2], "seq", split_axis=0, concat_axis=1, tiled=True),
    )
    results = [
        back.reshape(tokens_here, HEADS, 2, HEAD_DIM)
        .sum(axis=2)
        .astype(jnp.bfloat16)
        .reshape(tokens_here, full_width)
        for back in returned
    ]
    return (results[0], results[1], results[2])


MESH = pl.DeviceIdType.MESH
QUERY_TILE = 256
LOG2E = 1.4426950408889634
NEVER = -1e30


def fused_kernel(
    count,
    per_device,
    k_in,
    v_in,
    q_in,
    d_in,
    vertical,
    slash_offsets,
    counts,
    dq_out,
    dk_out,
    dv_out,
    arrived,
    finished,
    bias,
    key_acc,
    value_acc,
    fwd_send,
    fwd_recv,
    fwd_local,
    back_send,
    back_recv,
    back_local,
):
    me = lax.axis_index("seq")
    sources = (k_in, v_in, q_in, d_in)
    targets = (dk_out, dv_out, dq_out)
    length = count * BLK
    score_scale = HEAD_DIM ** (-0.5)

    def offset_of(step):
        return count // 2 + ((step + 1) // 2) * (2 * (step % 2) - 1)

    def rows_of(index):
        return pl.ds(pl.multiple_of(index * BLK, BLK), BLK)

    def columns_of(owner, slot):
        return pl.ds(pl.multiple_of((owner * per_device + slot) * HEAD_DIM, HEAD_DIM), HEAD_DIM)

    def forward(which, slot, step, sending):
        peer = lax.rem(me + offset_of(step), count)
        source = lax.rem(me + count - offset_of(step), count)
        return pltpu.make_async_remote_copy(
            src_ref=sources[which].at[:, columns_of(peer, slot)],
            dst_ref=arrived.at[which, slot, rows_of(me if sending else source), :],
            send_sem=fwd_send.at[which, slot, step],
            recv_sem=fwd_recv.at[which, slot, step],
            device_id={"seq": peer},
            device_id_type=MESH,
        )

    def own_forward(which, slot):
        return pltpu.make_async_copy(
            sources[which].at[:, columns_of(me, slot)],
            arrived.at[which, slot, rows_of(me), :],
            fwd_local.at[which, slot],
        )

    def backward(which, slot, step, sending):
        peer = lax.rem(me + offset_of(step), count)
        source = lax.rem(me + count - offset_of(step), count)
        return pltpu.make_async_remote_copy(
            src_ref=finished.at[which, slot, rows_of(peer), :],
            dst_ref=targets[which].at[:, columns_of(me if sending else source, slot)],
            send_sem=back_send.at[which, slot, step],
            recv_sem=back_recv.at[which, slot, step],
            device_id={"seq": peer},
            device_id_type=MESH,
        )

    def own_backward(which, slot):
        return pltpu.make_async_copy(
            finished.at[which, slot, rows_of(me), :],
            targets[which].at[:, columns_of(me, slot)],
            back_local.at[which, slot],
        )

    def each_step(do):
        @pl.loop(0, count - 1)
        def _(step):
            do(step)

    barrier = pltpu.get_barrier_semaphore()

    @pl.loop(1, count)
    def _(step):
        pl.semaphore_signal(
            barrier, inc=1, device_id={"seq": lax.rem(me + step, count)}, device_id_type=MESH
        )

    pl.semaphore_wait(barrier, count - 1)

    for slot in range(per_device):

        def send_all(step, slot=slot):
            for which in range(4):
                if slot > 0:
                    forward(which, slot - 1, step, True).wait_send()
                forward(which, slot, step, True).start()

        each_step(send_all)
        for which in range(4):
            own_forward(which, slot).start()

    query_block = lax.broadcasted_iota(jnp.int32, (count, length), 0)
    key_block = lax.broadcasted_iota(jnp.int32, (count, length), 1) // BLK
    for slot in range(per_device):
        head = me * per_device + slot
        allowed = jnp.zeros((count, length), jnp.float32)
        for entry in range(vertical.shape[0]):
            wanted = jnp.where(entry < counts[0, head], vertical[entry, head], -1)
            allowed = jnp.where(key_block == wanted, 1.0, allowed)
        for entry in range(slash_offsets.shape[0]):
            wanted = jnp.where(entry < counts[1, head], slash_offsets[entry, head], 2 * count)
            allowed = jnp.where(query_block - key_block == wanted, 1.0, allowed)
        bias[slot] = jnp.where(allowed > 0.0, 0.0, NEVER)

    def dot(a, b, a_dim, b_dim):
        return lax.dot_general(
            a, b, (((a_dim,), (b_dim,)), ((), ())), preferred_element_type=jnp.float32
        )

    def give_back(slot):
        def send_back(step):
            for which in range(3):
                backward(which, slot, step, True).start()

        each_step(send_back)
        for which in range(3):
            own_backward(which, slot).start()

    for slot in range(per_device):

        def arrive(step, slot=slot):
            for which in range(4):
                forward(which, slot, step, False).wait_recv()

        each_step(arrive)
        for which in range(4):
            own_forward(which, slot).wait()
        if slot > 0:
            give_back(slot - 1)

        key_acc[...] = jnp.zeros_like(key_acc)
        value_acc[...] = jnp.zeros_like(value_acc)

        @pl.loop(0, length // QUERY_TILE)
        def _(tile, slot=slot):
            rows = pl.ds(pl.multiple_of(tile * QUERY_TILE, QUERY_TILE), QUERY_TILE)
            keys = arrived[0, slot]
            values = arrived[1, slot]
            q_tile = arrived[2, slot, rows, :]
            d_tile = arrived[3, slot, rows, :]
            blocks_here = QUERY_TILE // BLK
            mask = jnp.concatenate(
                [
                    jnp.broadcast_to(
                        bias[slot, pl.ds(tile * blocks_here + part, 1), :], (BLK, length)
                    )
                    for part in range(blocks_here)
                ],
                axis=0,
            )
            scores = dot(q_tile, keys, 1, 1) * (score_scale * LOG2E) + mask
            top = jnp.max(scores, axis=-1, keepdims=True)
            raised = jnp.exp2(scores - top)
            total = jnp.sum(raised, axis=-1, keepdims=True)
            probs = raised * (1.0 / total)
            weights = probs.astype(jnp.bfloat16)
            attended = dot(weights, values, 1, 0)
            row_delta = jnp.sum(d_tile.astype(jnp.float32) * attended, axis=-1, keepdims=True)
            grad_probs = dot(d_tile, values, 1, 1)
            grad_scores = (probs * (grad_probs - row_delta)).astype(jnp.bfloat16)
            finished[2, slot, rows, :] = (dot(grad_scores, keys, 1, 0) * score_scale).astype(
                jnp.bfloat16
            )
            key_acc[...] += dot(q_tile, grad_scores, 0, 0)
            value_acc[...] += dot(d_tile, weights, 0, 0)

        finished[0, slot] = (key_acc[...] * score_scale).T.astype(jnp.bfloat16)
        finished[1, slot] = value_acc[...].T.astype(jnp.bfloat16)

    give_back(per_device - 1)

    for slot in range(per_device):

        def drain(step, slot=slot):
            if slot == per_device - 1:
                for which in range(4):
                    forward(which, slot, step, True).wait_send()
            for which in range(3):
                backward(which, slot, step, True).wait_send()
                backward(which, slot, step, False).wait_recv()

        each_step(drain)
        for which in range(3):
            own_backward(which, slot).wait()


def store_kernel(dq_in, dk_in, dv_in, dq_out, dk_out, dv_out):
    dq_out[...] = dq_in[...]
    dk_out[...] = dk_in[...]
    dv_out[...] = dv_in[...]


def whole_head_body(queries, key_rows, value_rows, out_grad, vertical, slash_offsets, counts):
    count = lax.axis_size("seq")
    per_device = HEADS // count
    length = count * BLK
    anywhere = pl.BlockSpec(memory_space=pl.ANY)
    scalars = pl.BlockSpec(memory_space=pltpu.SMEM)
    shape = jax.ShapeDtypeStruct(queries.shape, queries.dtype)
    sems = pltpu.SemaphoreType.DMA
    query_grad, key_grad, value_grad = pl.pallas_call(
        functools.partial(fused_kernel, count, per_device),
        out_shape=(shape, shape, shape),
        in_specs=[anywhere] * 4 + [scalars] * 3,
        out_specs=(anywhere, anywhere, anywhere),
        scratch_shapes=[
            pltpu.VMEM((4, per_device, length, HEAD_DIM), jnp.bfloat16),
            pltpu.VMEM((3, per_device, length, HEAD_DIM), jnp.bfloat16),
            pltpu.VMEM((per_device, count, length), jnp.float32),
            pltpu.VMEM((HEAD_DIM, length), jnp.float32),
            pltpu.VMEM((HEAD_DIM, length), jnp.float32),
            sems((4, per_device, count - 1)),
            sems((4, per_device, count - 1)),
            sems((4, per_device)),
            sems((3, per_device, count - 1)),
            sems((3, per_device, count - 1)),
            sems((3, per_device)),
        ],
        compiler_params=pltpu.CompilerParams(
            collective_id=0, has_side_effects=True, vmem_limit_bytes=64 * 1024 * 1024
        ),
    )(key_rows, value_rows, queries, out_grad, vertical.T, slash_offsets.T, counts.T)
    width = queries.shape[1] // 4
    block = pl.BlockSpec((queries.shape[0], width), lambda part: (0, part))
    return pl.pallas_call(
        store_kernel,
        grid=(4,),
        out_shape=(shape, shape, shape),
        in_specs=[block] * 3,
        out_specs=(block,) * 3,
        compiler_params=pltpu.CompilerParams(vmem_limit_bytes=64 * 1024 * 1024),
    )(query_grad, key_grad, value_grad)


def solution(mesh):
    whole_heads = HEADS % mesh.shape["seq"] == 0
    return jax.shard_map(
        whole_head_body if whole_heads else split_head_body,
        mesh=mesh,
        in_specs=(
            P(("doc", "seq"), None),
            P(("doc", "seq"), None),
            P(("doc", "seq"), None),
            P(("doc", "seq"), None),
            P("doc", None),
            P("doc", None),
            P("doc", None),
        ),
        out_specs=(P(("doc", "seq"), None), P(("doc", "seq"), None), P(("doc", "seq"), None)),
        check_vma=False,
    )
```

```python
import functools

import jax
import jax.numpy as jnp
from jax import lax
from jax.experimental import pallas as pl
from jax.experimental.pallas import tpu as pltpu
from jax.sharding import PartitionSpec as P

HEADS = 16
HEAD_DIM = 128
BLK = 128


block_group = 4


def block_lists(chosen, vert_head, slash_head, count_head, nblocks):
    vert_cap = vert_head.shape[0]
    slash_cap = slash_head.shape[0]
    rows_now = chosen.shape[0]
    vert_index = jnp.broadcast_to(vert_head[None, :], (rows_now, vert_cap))
    vert_valid = jnp.broadcast_to(
        (jnp.arange(vert_cap, dtype=jnp.int32) < count_head[0])[None, :], (rows_now, vert_cap)
    )
    slash_index = chosen[:, None] - slash_head[None, :]
    inside = (slash_index >= 0) & (slash_index < nblocks)
    repeated = jnp.any(
        (vert_index[:, :, None] == slash_index[:, None, :]) & vert_valid[:, :, None], axis=1
    )
    slash_valid = (
        (jnp.arange(slash_cap, dtype=jnp.int32) < count_head[1])[None, :]
        & inside
        & jnp.logical_not(repeated)
    )
    index_table = jnp.clip(jnp.concatenate([vert_index, slash_index], axis=1), 0, nblocks - 1)
    valid_table = jnp.concatenate([vert_valid, slash_valid], axis=1)
    return (index_table, valid_table)


def owner_backward(
    q_blocks, k_blocks, v_blocks, d_blocks, vert_head, slash_head, count_head, chosen_all
):
    nblocks, blk_rows, head_dim = q_blocks.shape
    score_scale = head_dim ** (-0.5)
    vert_cap = vert_head.shape[0]
    trips = count_head[0] + count_head[1]

    def one_group(carried, chosen):
        key_acc, value_acc = carried
        index_table, valid_table = block_lists(chosen, vert_head, slash_head, count_head, nblocks)
        q_group = q_blocks[chosen]
        d_group = d_blocks[chosen]
        group_shape = (chosen.shape[0], blk_rows, 1)

        def fetch(position):
            slot_pick = jnp.where(
                position < count_head[0], position, vert_cap + position - count_head[0]
            )
            column = lax.dynamic_index_in_dim(index_table, slot_pick, 1, keepdims=False)
            usable = lax.dynamic_index_in_dim(valid_table, slot_pick, 1, keepdims=False)[
                :, None, None
            ]
            k_tile = k_blocks[column]
            v_tile = v_blocks[column]
            scores = (
                jnp.einsum("gqd,gkd->gqk", q_group, k_tile, preferred_element_type=jnp.float32)
                * score_scale
            )
            return (column, usable, k_tile, v_tile, scores)

        def row_stats(position, running):
            row_top, row_total = running
            column, usable, k_tile, v_tile, scores = fetch(position)
            new_top = jnp.maximum(
                row_top, jnp.where(usable, jnp.max(scores, axis=-1, keepdims=True), -1e30)
            )
            added = jnp.where(
                usable, jnp.sum(jnp.exp(scores - new_top), axis=-1, keepdims=True), 0.0
            )
            return (new_top, row_total * jnp.exp(row_top - new_top) + added)

        row_top, row_total = lax.fori_loop(
            0,
            trips,
            row_stats,
            (jnp.full(group_shape, -1e30, jnp.float32), jnp.zeros(group_shape, jnp.float32)),
        )

        def probs_of(scores, usable):
            return jnp.where(usable, jnp.exp(scores - row_top) / row_total, 0.0)

        def output_step(position, running):
            column, usable, k_tile, v_tile, scores = fetch(position)
            weights = probs_of(scores, usable).astype(jnp.bfloat16)
            return running + jnp.einsum(
                "gqk,gkd->gqd", weights, v_tile, preferred_element_type=jnp.float32
            )

        attended = lax.fori_loop(
            0, trips, output_step, jnp.zeros((chosen.shape[0], blk_rows, head_dim), jnp.float32)
        )
        row_delta = jnp.sum(d_group.astype(jnp.float32) * attended, axis=-1, keepdims=True)

        def grad_step(position, running):
            query_acc, key_run, value_run = running
            column, usable, k_tile, v_tile, scores = fetch(position)
            probs = probs_of(scores, usable)
            weights = probs.astype(jnp.bfloat16)
            grad_probs = jnp.einsum(
                "gqd,gkd->gqk", d_group, v_tile, preferred_element_type=jnp.float32
            )
            grad_scores = (probs * (grad_probs - row_delta)).astype(jnp.bfloat16)
            query_acc = query_acc + jnp.einsum(
                "gqk,gkd->gqd", grad_scores, k_tile, preferred_element_type=jnp.float32
            )
            key_part = (
                jnp.einsum("gqk,gqd->gkd", grad_scores, q_group, preferred_element_type=jnp.float32)
                * score_scale
            )
            value_part = jnp.einsum(
                "gqk,gqd->gkd", weights, d_group, preferred_element_type=jnp.float32
            )
            return (
                query_acc,
                key_run.at[column].add(key_part),
                value_run.at[column].add(value_part),
            )

        start_query = jnp.zeros((chosen.shape[0], blk_rows, head_dim), jnp.float32)
        query_acc, key_acc, value_acc = lax.fori_loop(
            0, trips, grad_step, (start_query, key_acc, value_acc)
        )
        return ((key_acc, value_acc), query_acc * score_scale)

    zeros_acc = jnp.zeros((nblocks, blk_rows, head_dim), jnp.float32)
    (key_acc, value_acc), query_grad = lax.scan(one_group, (zeros_acc, zeros_acc), chosen_all)
    return (query_grad.reshape(-1, blk_rows, head_dim), key_acc, value_acc)


def split_head_body(queries, key_rows, value_rows, out_grad, vertical, slash_offsets, counts):
    tokens_here = queries.shape[0]
    device_count = lax.axis_size("seq")
    device_here = lax.axis_index("seq")
    full_width = HEADS * HEAD_DIM

    def doubled(matrix):
        return jnp.repeat(matrix.reshape(tokens_here, HEADS, HEAD_DIM), 2, axis=1)

    q_owned, k_owned, v_owned, d_owned = (
        lax.all_to_all(doubled(queries), "seq", split_axis=1, concat_axis=0, tiled=True),
        lax.all_to_all(doubled(key_rows), "seq", split_axis=1, concat_axis=0, tiled=True),
        lax.all_to_all(doubled(value_rows), "seq", split_axis=1, concat_axis=0, tiled=True),
        lax.all_to_all(doubled(out_grad), "seq", split_axis=1, concat_axis=0, tiled=True),
    )
    length = tokens_here * device_count
    nblocks = length // BLK
    per_device = 2 * HEADS // device_count
    query_parts = []
    key_parts = []
    value_parts = []
    for local_slot in range(per_device):
        slot_index = device_here * per_device + local_slot
        head_index = slot_index // 2
        parity = slot_index % 2
        chosen_all = (parity + 2 * jnp.arange(nblocks // 2, dtype=jnp.int32)).reshape(
            -1, block_group
        )

        def blockwise(matrix):
            return matrix[:, local_slot, :].reshape(nblocks, BLK, HEAD_DIM)

        query_sel, key_acc, value_acc = owner_backward(
            blockwise(q_owned),
            blockwise(k_owned),
            blockwise(v_owned),
            blockwise(d_owned),
            vertical[head_index],
            slash_offsets[head_index],
            counts[head_index],
            chosen_all,
        )
        query_full = (
            jnp.zeros((nblocks, BLK, HEAD_DIM), jnp.float32)
            .at[chosen_all.reshape(-1)]
            .set(query_sel)
        )
        query_parts.append(query_full.reshape(length, HEAD_DIM))
        key_parts.append(key_acc.reshape(length, HEAD_DIM))
        value_parts.append(value_acc.reshape(length, HEAD_DIM))
    all_parts = (query_parts, key_parts, value_parts)
    stacked = [jnp.stack(member, axis=1) for member in all_parts]
    returned = (
        lax.all_to_all(stacked[0], "seq", split_axis=0, concat_axis=1, tiled=True),
        lax.all_to_all(stacked[1], "seq", split_axis=0, concat_axis=1, tiled=True),
        lax.all_to_all(stacked[2], "seq", split_axis=0, concat_axis=1, tiled=True),
    )
    results = [
        back.reshape(tokens_here, HEADS, 2, HEAD_DIM)
        .sum(axis=2)
        .astype(jnp.bfloat16)
        .reshape(tokens_here, full_width)
        for back in returned
    ]
    return (results[0], results[1], results[2])


MESH = pl.DeviceIdType.MESH
QUERY_TILE = 256
LOG2E = 1.4426950408889634
NEVER = -1e30


def fused_kernel(
    count,
    slots,
    k_in,
    v_in,
    q_in,
    d_in,
    vertical,
    slash_offsets,
    counts,
    dq_parts,
    dk_out,
    dv_out,
    kv_here,
    qd_here,
    dkv_done,
    dq_done,
    bias,
    stats,
    partner_stats,
    key_acc,
    value_acc,
    kv_send,
    kv_recv,
    qd_send,
    qd_recv,
    own_in,
    stat_send,
    stat_recv,
    dkv_send,
    dkv_recv,
    dq_send,
    dq_recv,
    own_back,
):
    me = lax.axis_index("seq")
    near = count // 2
    half = me // near
    group = me % near
    first = half * near
    length = count * BLK
    score_scale = HEAD_DIM ** (-0.5)
    kv_sources = (k_in, v_in)
    qd_sources = (q_in, d_in)
    dkv_targets = (dk_out, dv_out)

    def offset_of(step):
        return count // 2 + ((step + 1) // 2) * (2 * (step % 2) - 1)

    def rows_of(index):
        return pl.ds(pl.multiple_of(index * BLK, BLK), BLK)

    def columns_of(owner_group, slot):
        return pl.ds(pl.multiple_of((owner_group * slots + slot) * HEAD_DIM, HEAD_DIM), HEAD_DIM)

    def far_pair(step):
        offset = offset_of(step)
        return (me + offset) % count, (me + count - offset) % count

    def near_pair(step):
        return (group + 1 + step) % near, (group + near - 1 - step) % near

    def remote(src, dst, send_sem, recv_sem, peer):
        return pltpu.make_async_remote_copy(
            src_ref=src,
            dst_ref=dst,
            send_sem=send_sem,
            recv_sem=recv_sem,
            device_id={"seq": peer},
            device_id_type=MESH,
        )

    def send_qd(which, slot, step, sending):
        peer, source = far_pair(step)
        return remote(
            qd_sources[which].at[:, columns_of(peer % near, slot)],
            qd_here.at[which, slot, rows_of(me if sending else source), :],
            qd_send.at[which, slot, step],
            qd_recv.at[which, slot, step],
            peer,
        )

    def send_kv(which, slot, step, sending):
        peer, source = near_pair(step)
        return remote(
            kv_sources[which].at[:, columns_of(peer, slot)],
            kv_here.at[which, slot, rows_of(group if sending else source), :],
            kv_send.at[which, slot, step],
            kv_recv.at[which, slot, step],
            first + peer,
        )

    def own_copies(slot):
        here = columns_of(group, slot)
        pairs = [
            (kv_sources[which].at[:, here], kv_here.at[which, slot, rows_of(group), :])
            for which in range(2)
        ] + [
            (qd_sources[which].at[:, here], qd_here.at[which, slot, rows_of(me), :])
            for which in range(2)
        ]
        return [
            pltpu.make_async_copy(src, dst, own_in.at[index, slot])
            for index, (src, dst) in enumerate(pairs)
        ]

    def send_stats(slot):
        return remote(
            stats.at[slot],
            partner_stats.at[slot],
            stat_send.at[slot],
            stat_recv.at[slot],
            (me + near) % count,
        )

    def back_dq(slot, step, sending):
        peer, source = far_pair(step)
        origin = me if sending else source
        return remote(
            dq_done.at[slot, rows_of(peer), :],
            dq_parts.at[rows_of(origin // near), columns_of(origin % near, slot)],
            dq_send.at[slot, step],
            dq_recv.at[slot, step],
            peer,
        )

    def back_dkv(which, slot, step, sending):
        peer, source = near_pair(step)
        return remote(
            dkv_done.at[which, slot, rows_of(peer), :],
            dkv_targets[which].at[:, columns_of(group if sending else source, slot)],
            dkv_send.at[which, slot, step],
            dkv_recv.at[which, slot, step],
            first + peer,
        )

    def own_returns(slot):
        here = columns_of(group, slot)
        pairs = [
            (dkv_done.at[which, slot, rows_of(group), :], dkv_targets[which].at[:, here])
            for which in range(2)
        ] + [(dq_done.at[slot, rows_of(me), :], dq_parts.at[rows_of(half), here])]
        return [
            pltpu.make_async_copy(src, dst, own_back.at[index, slot])
            for index, (src, dst) in enumerate(pairs)
        ]

    barrier = pltpu.get_barrier_semaphore()

    @pl.loop(1, count)
    def _(step):
        pl.semaphore_signal(
            barrier, inc=1, device_id={"seq": (me + step) % count}, device_id_type=MESH
        )

    pl.semaphore_wait(barrier, count - 1)

    for slot in range(slots):

        @pl.loop(0, count - 1)
        def _(step, slot=slot):
            for which in range(2):
                send_qd(which, slot, step, True).start()

        @pl.loop(0, near - 1)
        def _(step, slot=slot):
            for which in range(2):
                send_kv(which, slot, step, True).start()

        for copy in own_copies(slot):
            copy.start()

    key_block = first + lax.broadcasted_iota(jnp.int32, (near, length), 0)
    query_block = lax.broadcasted_iota(jnp.int32, (near, length), 1) // BLK
    for slot in range(slots):
        head = group * slots + slot
        allowed = jnp.zeros((near, length), jnp.float32)
        for entry in range(vertical.shape[0]):
            wanted = jnp.where(entry < counts[0, head], vertical[entry, head], -1)
            allowed = jnp.where(key_block == wanted, 1.0, allowed)
        for entry in range(slash_offsets.shape[0]):
            wanted = jnp.where(entry < counts[1, head], slash_offsets[entry, head], 2 * count)
            allowed = jnp.where(query_block - key_block == wanted, 1.0, allowed)
        bias[slot] = jnp.where(allowed > 0.0, 0.0, NEVER)

    def dot(a, b, a_dim, b_dim):
        return lax.dot_general(
            a, b, (((a_dim,), (b_dim,)), ((), ())), preferred_element_type=jnp.float32
        )

    def tile_range(tile):
        return pl.ds(pl.multiple_of(tile * QUERY_TILE, QUERY_TILE), QUERY_TILE)

    def scores_of(slot, here):
        mask = jnp.concatenate(
            [
                jnp.broadcast_to(bias[slot, part : part + 1, here], (BLK, QUERY_TILE))
                for part in range(near)
            ],
            axis=0,
        )
        products = dot(kv_here[0, slot], qd_here[0, slot, here, :], 1, 1)
        return products * (score_scale * LOG2E) + mask

    def first_phase(slot):
        @pl.loop(0, count - 1)
        def _(step):
            for which in range(2):
                send_qd(which, slot, step, False).wait_recv()

        @pl.loop(0, near - 1)
        def _(step):
            for which in range(2):
                send_kv(which, slot, step, False).wait_recv()

        for copy in own_copies(slot):
            copy.wait()

        @pl.loop(0, length // QUERY_TILE)
        def _(tile):
            here = tile_range(tile)
            scores = scores_of(slot, here)
            top = jnp.max(scores, axis=0, keepdims=True)
            raised = jnp.exp2(scores - top)
            grad_probs = dot(kv_here[1, slot], qd_here[1, slot, here, :], 1, 1)
            stats[slot, 0, :, here] = top
            stats[slot, 1, :, here] = jnp.sum(raised, axis=0, keepdims=True)
            stats[slot, 2, :, here] = jnp.sum(raised * grad_probs, axis=0, keepdims=True)

        send_stats(slot).start()

    def second_phase(slot):
        send_stats(slot).wait_recv()
        key_acc[...] = jnp.zeros_like(key_acc)
        value_acc[...] = jnp.zeros_like(value_acc)

        @pl.loop(0, length // QUERY_TILE)
        def _(tile):
            here = tile_range(tile)
            keys = kv_here[0, slot]
            q_tile = qd_here[0, slot, here, :]
            d_tile = qd_here[1, slot, here, :]
            my_top = stats[slot, 0, :, here]
            its_top = partner_stats[slot, 0, :, here]
            top = jnp.maximum(my_top, its_top)
            mine = jnp.exp2(my_top - top)
            its = jnp.exp2(its_top - top)
            inverse = 1.0 / (stats[slot, 1, :, here] * mine + partner_stats[slot, 1, :, here] * its)
            row_delta = inverse * (
                stats[slot, 2, :, here] * mine + partner_stats[slot, 2, :, here] * its
            )
            probs = jnp.exp2(scores_of(slot, here) - top) * inverse
            weights = probs.astype(jnp.bfloat16)
            grad_probs = dot(kv_here[1, slot], d_tile, 1, 1)
            grad_scores = (probs * (grad_probs - row_delta)).astype(jnp.bfloat16)
            dq_done[slot, here, :] = (dot(keys, grad_scores, 0, 0) * score_scale).T.astype(
                jnp.bfloat16
            )
            key_acc[...] += dot(grad_scores, q_tile, 1, 0)
            value_acc[...] += dot(weights, d_tile, 1, 0)

        dkv_done[0, slot] = (key_acc[...] * score_scale).astype(jnp.bfloat16)
        dkv_done[1, slot] = value_acc[...].astype(jnp.bfloat16)

        @pl.loop(0, count - 1)
        def _(step):
            back_dq(slot, step, True).start()

        @pl.loop(0, near - 1)
        def _(step):
            for which in range(2):
                back_dkv(which, slot, step, True).start()

        for copy in own_returns(slot):
            copy.start()

    for slot in range(slots):
        first_phase(slot)
        if slot > 0:
            second_phase(slot - 1)
    second_phase(slots - 1)

    for slot in range(slots):

        @pl.loop(0, count - 1)
        def _(step, slot=slot):
            for which in range(2):
                send_qd(which, slot, step, True).wait_send()
            back_dq(slot, step, True).wait_send()
            back_dq(slot, step, False).wait_recv()

        @pl.loop(0, near - 1)
        def _(step, slot=slot):
            for which in range(2):
                send_kv(which, slot, step, True).wait_send()
                back_dkv(which, slot, step, True).wait_send()
                back_dkv(which, slot, step, False).wait_recv()

        send_stats(slot).wait_send()
        for copy in own_returns(slot):
            copy.wait()


def whole_head_body(queries, key_rows, value_rows, out_grad, vertical, slash_offsets, counts):
    count = lax.axis_size("seq")
    near = count // 2
    slots = HEADS // near
    length = count * BLK
    kept = near * BLK
    anywhere = pl.BlockSpec(memory_space=pl.ANY)
    scalars = pl.BlockSpec(memory_space=pltpu.SMEM)
    shape = jax.ShapeDtypeStruct(queries.shape, queries.dtype)
    parts = jax.ShapeDtypeStruct((2 * queries.shape[0], queries.shape[1]), queries.dtype)
    sems = pltpu.SemaphoreType.DMA
    dq_parts, key_grad, value_grad = pl.pallas_call(
        functools.partial(fused_kernel, count, slots),
        out_shape=(parts, shape, shape),
        in_specs=[anywhere] * 4 + [scalars] * 3,
        out_specs=(anywhere, anywhere, anywhere),
        scratch_shapes=[
            pltpu.VMEM((2, slots, kept, HEAD_DIM), jnp.bfloat16),
            pltpu.VMEM((2, slots, length, HEAD_DIM), jnp.bfloat16),
            pltpu.VMEM((2, slots, kept, HEAD_DIM), jnp.bfloat16),
            pltpu.VMEM((slots, length, HEAD_DIM), jnp.bfloat16),
            pltpu.VMEM((slots, near, length), jnp.float32),
            pltpu.VMEM((slots, 3, 1, length), jnp.float32),
            pltpu.VMEM((slots, 3, 1, length), jnp.float32),
            pltpu.VMEM((kept, HEAD_DIM), jnp.float32),
            pltpu.VMEM((kept, HEAD_DIM), jnp.float32),
            sems((2, slots, near - 1)),
            sems((2, slots, near - 1)),
            sems((2, slots, count - 1)),
            sems((2, slots, count - 1)),
            sems((4, slots)),
            sems((slots,)),
            sems((slots,)),
            sems((2, slots, near - 1)),
            sems((2, slots, near - 1)),
            sems((slots, count - 1)),
            sems((slots, count - 1)),
            sems((3, slots)),
        ],
        compiler_params=pltpu.CompilerParams(
            collective_id=0, has_side_effects=True, vmem_limit_bytes=64 * 1024 * 1024
        ),
    )(key_rows, value_rows, queries, out_grad, vertical.T, slash_offsets.T, counts.T)
    rows = queries.shape[0]
    query_grad = dq_parts[:rows].astype(jnp.float32) + dq_parts[rows:].astype(jnp.float32)
    return query_grad.astype(queries.dtype), key_grad, value_grad


def solution(mesh):
    whole_heads = HEADS % mesh.shape["seq"] == 0
    return jax.shard_map(
        whole_head_body if whole_heads else split_head_body,
        mesh=mesh,
        in_specs=(
            P(("doc", "seq"), None),
            P(("doc", "seq"), None),
            P(("doc", "seq"), None),
            P(("doc", "seq"), None),
            P("doc", None),
            P("doc", None),
            P("doc", None),
        ),
        out_specs=(P(("doc", "seq"), None), P(("doc", "seq"), None), P(("doc", "seq"), None)),
        check_vma=False,
    )
```

```python
import functools

import jax
import jax.numpy as jnp
from jax import lax
from jax.experimental import pallas as pl
from jax.experimental.pallas import tpu as pltpu
from jax.sharding import PartitionSpec as P

HEADS = 16
HEAD_DIM = 128
BLK = 128


block_group = 4


def block_lists(chosen, vert_head, slash_head, count_head, nblocks):
    vert_cap = vert_head.shape[0]
    slash_cap = slash_head.shape[0]
    rows_now = chosen.shape[0]
    vert_index = jnp.broadcast_to(vert_head[None, :], (rows_now, vert_cap))
    vert_valid = jnp.broadcast_to(
        (jnp.arange(vert_cap, dtype=jnp.int32) < count_head[0])[None, :], (rows_now, vert_cap)
    )
    slash_index = chosen[:, None] - slash_head[None, :]
    inside = (slash_index >= 0) & (slash_index < nblocks)
    repeated = jnp.any(
        (vert_index[:, :, None] == slash_index[:, None, :]) & vert_valid[:, :, None], axis=1
    )
    slash_valid = (
        (jnp.arange(slash_cap, dtype=jnp.int32) < count_head[1])[None, :]
        & inside
        & jnp.logical_not(repeated)
    )
    index_table = jnp.clip(jnp.concatenate([vert_index, slash_index], axis=1), 0, nblocks - 1)
    valid_table = jnp.concatenate([vert_valid, slash_valid], axis=1)
    return (index_table, valid_table)


def owner_backward(
    q_blocks, k_blocks, v_blocks, d_blocks, vert_head, slash_head, count_head, chosen_all
):
    nblocks, blk_rows, head_dim = q_blocks.shape
    score_scale = head_dim ** (-0.5)
    vert_cap = vert_head.shape[0]
    trips = count_head[0] + count_head[1]

    def one_group(carried, chosen):
        key_acc, value_acc = carried
        index_table, valid_table = block_lists(chosen, vert_head, slash_head, count_head, nblocks)
        q_group = q_blocks[chosen]
        d_group = d_blocks[chosen]
        group_shape = (chosen.shape[0], blk_rows, 1)

        def fetch(position):
            slot_pick = jnp.where(
                position < count_head[0], position, vert_cap + position - count_head[0]
            )
            column = lax.dynamic_index_in_dim(index_table, slot_pick, 1, keepdims=False)
            usable = lax.dynamic_index_in_dim(valid_table, slot_pick, 1, keepdims=False)[
                :, None, None
            ]
            k_tile = k_blocks[column]
            v_tile = v_blocks[column]
            scores = (
                jnp.einsum("gqd,gkd->gqk", q_group, k_tile, preferred_element_type=jnp.float32)
                * score_scale
            )
            return (column, usable, k_tile, v_tile, scores)

        def row_stats(position, running):
            row_top, row_total = running
            column, usable, k_tile, v_tile, scores = fetch(position)
            new_top = jnp.maximum(
                row_top, jnp.where(usable, jnp.max(scores, axis=-1, keepdims=True), -1e30)
            )
            added = jnp.where(
                usable, jnp.sum(jnp.exp(scores - new_top), axis=-1, keepdims=True), 0.0
            )
            return (new_top, row_total * jnp.exp(row_top - new_top) + added)

        row_top, row_total = lax.fori_loop(
            0,
            trips,
            row_stats,
            (jnp.full(group_shape, -1e30, jnp.float32), jnp.zeros(group_shape, jnp.float32)),
        )

        def probs_of(scores, usable):
            return jnp.where(usable, jnp.exp(scores - row_top) / row_total, 0.0)

        def output_step(position, running):
            column, usable, k_tile, v_tile, scores = fetch(position)
            weights = probs_of(scores, usable).astype(jnp.bfloat16)
            return running + jnp.einsum(
                "gqk,gkd->gqd", weights, v_tile, preferred_element_type=jnp.float32
            )

        attended = lax.fori_loop(
            0, trips, output_step, jnp.zeros((chosen.shape[0], blk_rows, head_dim), jnp.float32)
        )
        row_delta = jnp.sum(d_group.astype(jnp.float32) * attended, axis=-1, keepdims=True)

        def grad_step(position, running):
            query_acc, key_run, value_run = running
            column, usable, k_tile, v_tile, scores = fetch(position)
            probs = probs_of(scores, usable)
            weights = probs.astype(jnp.bfloat16)
            grad_probs = jnp.einsum(
                "gqd,gkd->gqk", d_group, v_tile, preferred_element_type=jnp.float32
            )
            grad_scores = (probs * (grad_probs - row_delta)).astype(jnp.bfloat16)
            query_acc = query_acc + jnp.einsum(
                "gqk,gkd->gqd", grad_scores, k_tile, preferred_element_type=jnp.float32
            )
            key_part = (
                jnp.einsum("gqk,gqd->gkd", grad_scores, q_group, preferred_element_type=jnp.float32)
                * score_scale
            )
            value_part = jnp.einsum(
                "gqk,gqd->gkd", weights, d_group, preferred_element_type=jnp.float32
            )
            return (
                query_acc,
                key_run.at[column].add(key_part),
                value_run.at[column].add(value_part),
            )

        start_query = jnp.zeros((chosen.shape[0], blk_rows, head_dim), jnp.float32)
        query_acc, key_acc, value_acc = lax.fori_loop(
            0, trips, grad_step, (start_query, key_acc, value_acc)
        )
        return ((key_acc, value_acc), query_acc * score_scale)

    zeros_acc = jnp.zeros((nblocks, blk_rows, head_dim), jnp.float32)
    (key_acc, value_acc), query_grad = lax.scan(one_group, (zeros_acc, zeros_acc), chosen_all)
    return (query_grad.reshape(-1, blk_rows, head_dim), key_acc, value_acc)


def split_head_body(queries, key_rows, value_rows, out_grad, vertical, slash_offsets, counts):
    tokens_here = queries.shape[0]
    device_count = lax.axis_size("seq")
    device_here = lax.axis_index("seq")
    full_width = HEADS * HEAD_DIM

    def doubled(matrix):
        return jnp.repeat(matrix.reshape(tokens_here, HEADS, HEAD_DIM), 2, axis=1)

    q_owned, k_owned, v_owned, d_owned = (
        lax.all_to_all(doubled(queries), "seq", split_axis=1, concat_axis=0, tiled=True),
        lax.all_to_all(doubled(key_rows), "seq", split_axis=1, concat_axis=0, tiled=True),
        lax.all_to_all(doubled(value_rows), "seq", split_axis=1, concat_axis=0, tiled=True),
        lax.all_to_all(doubled(out_grad), "seq", split_axis=1, concat_axis=0, tiled=True),
    )
    length = tokens_here * device_count
    nblocks = length // BLK
    per_device = 2 * HEADS // device_count
    query_parts = []
    key_parts = []
    value_parts = []
    for local_slot in range(per_device):
        slot_index = device_here * per_device + local_slot
        head_index = slot_index // 2
        parity = slot_index % 2
        chosen_all = (parity + 2 * jnp.arange(nblocks // 2, dtype=jnp.int32)).reshape(
            -1, block_group
        )

        def blockwise(matrix):
            return matrix[:, local_slot, :].reshape(nblocks, BLK, HEAD_DIM)

        query_sel, key_acc, value_acc = owner_backward(
            blockwise(q_owned),
            blockwise(k_owned),
            blockwise(v_owned),
            blockwise(d_owned),
            vertical[head_index],
            slash_offsets[head_index],
            counts[head_index],
            chosen_all,
        )
        query_full = (
            jnp.zeros((nblocks, BLK, HEAD_DIM), jnp.float32)
            .at[chosen_all.reshape(-1)]
            .set(query_sel)
        )
        query_parts.append(query_full.reshape(length, HEAD_DIM))
        key_parts.append(key_acc.reshape(length, HEAD_DIM))
        value_parts.append(value_acc.reshape(length, HEAD_DIM))
    all_parts = (query_parts, key_parts, value_parts)
    stacked = [jnp.stack(member, axis=1) for member in all_parts]
    returned = (
        lax.all_to_all(stacked[0], "seq", split_axis=0, concat_axis=1, tiled=True),
        lax.all_to_all(stacked[1], "seq", split_axis=0, concat_axis=1, tiled=True),
        lax.all_to_all(stacked[2], "seq", split_axis=0, concat_axis=1, tiled=True),
    )
    results = [
        back.reshape(tokens_here, HEADS, 2, HEAD_DIM)
        .sum(axis=2)
        .astype(jnp.bfloat16)
        .reshape(tokens_here, full_width)
        for back in returned
    ]
    return (results[0], results[1], results[2])


MESH = pl.DeviceIdType.MESH
QUERY_TILE = 256
LOG2E = 1.4426950408889634
NEVER = -1e30


def fused_kernel(
    count,
    per_device,
    k_in,
    v_in,
    q_in,
    d_in,
    vertical,
    slash_offsets,
    counts,
    dq_out,
    dk_out,
    dv_out,
    arrived,
    finished,
    bias,
    key_acc,
    value_acc,
    fwd_send,
    fwd_recv,
    fwd_local,
    back_send,
    back_recv,
    back_local,
):
    me = lax.axis_index("seq")
    sources = (k_in, v_in, q_in, d_in)
    targets = (dk_out, dv_out, dq_out)
    length = count * BLK
    score_scale = HEAD_DIM ** (-0.5)

    def offset_of(step):
        return count // 2 + ((step + 1) // 2) * (2 * (step % 2) - 1)

    def rows_of(index):
        return pl.ds(pl.multiple_of(index * BLK, BLK), BLK)

    def columns_of(owner, slot):
        return pl.ds(pl.multiple_of((owner * per_device + slot) * HEAD_DIM, HEAD_DIM), HEAD_DIM)

    def forward(which, slot, step, sending):
        peer = lax.rem(me + offset_of(step), count)
        source = lax.rem(me + count - offset_of(step), count)
        return pltpu.make_async_remote_copy(
            src_ref=sources[which].at[:, columns_of(peer, slot)],
            dst_ref=arrived.at[which, slot, rows_of(me if sending else source), :],
            send_sem=fwd_send.at[which, slot, step],
            recv_sem=fwd_recv.at[which, slot, step],
            device_id={"seq": peer},
            device_id_type=MESH,
        )

    def own_forward(which, slot):
        return pltpu.make_async_copy(
            sources[which].at[:, columns_of(me, slot)],
            arrived.at[which, slot, rows_of(me), :],
            fwd_local.at[which, slot],
        )

    def backward(which, slot, step, sending):
        peer = lax.rem(me + offset_of(step), count)
        source = lax.rem(me + count - offset_of(step), count)
        return pltpu.make_async_remote_copy(
            src_ref=finished.at[which, slot, rows_of(peer), :],
            dst_ref=targets[which].at[:, columns_of(me if sending else source, slot)],
            send_sem=back_send.at[which, slot, step],
            recv_sem=back_recv.at[which, slot, step],
            device_id={"seq": peer},
            device_id_type=MESH,
        )

    def own_backward(which, slot):
        return pltpu.make_async_copy(
            finished.at[which, slot, rows_of(me), :],
            targets[which].at[:, columns_of(me, slot)],
            back_local.at[which, slot],
        )

    def each_step(do):
        @pl.loop(0, count - 1)
        def _(step):
            do(step)

    barrier = pltpu.get_barrier_semaphore()

    @pl.loop(1, count)
    def _(step):
        pl.semaphore_signal(
            barrier, inc=1, device_id={"seq": lax.rem(me + step, count)}, device_id_type=MESH
        )

    pl.semaphore_wait(barrier, count - 1)

    for slot in range(per_device):

        def send_all(step, slot=slot):
            for which in range(4):
                forward(which, slot, step, True).start()

        each_step(send_all)
        for which in range(4):
            own_forward(which, slot).start()

    query_block = lax.broadcasted_iota(jnp.int32, (count, length), 0)
    key_block = lax.broadcasted_iota(jnp.int32, (count, length), 1) // BLK
    for slot in range(per_device):
        head = me * per_device + slot
        allowed = jnp.zeros((count, length), jnp.float32)
        for entry in range(vertical.shape[0]):
            wanted = jnp.where(entry < counts[0, head], vertical[entry, head], -1)
            allowed = jnp.where(key_block == wanted, 1.0, allowed)
        for entry in range(slash_offsets.shape[0]):
            wanted = jnp.where(entry < counts[1, head], slash_offsets[entry, head], 2 * count)
            allowed = jnp.where(query_block - key_block == wanted, 1.0, allowed)
        bias[slot] = jnp.where(allowed > 0.0, 0.0, NEVER)

    def dot(a, b, a_dim, b_dim):
        return lax.dot_general(
            a, b, (((a_dim,), (b_dim,)), ((), ())), preferred_element_type=jnp.float32
        )

    for slot in range(per_device):

        def arrive(step, slot=slot):
            for which in range(4):
                forward(which, slot, step, False).wait_recv()

        each_step(arrive)
        for which in range(4):
            own_forward(which, slot).wait()

        key_acc[...] = jnp.zeros_like(key_acc)
        value_acc[...] = jnp.zeros_like(value_acc)

        @pl.loop(0, length // QUERY_TILE)
        def _(tile, slot=slot):
            rows = pl.ds(pl.multiple_of(tile * QUERY_TILE, QUERY_TILE), QUERY_TILE)
            keys = arrived[0, slot]
            values = arrived[1, slot]
            q_tile = arrived[2, slot, rows, :]
            d_tile = arrived[3, slot, rows, :]
            blocks_here = QUERY_TILE // BLK
            mask = jnp.concatenate(
                [
                    jnp.broadcast_to(
                        bias[slot, pl.ds(tile * blocks_here + part, 1), :], (BLK, length)
                    )
                    for part in range(blocks_here)
                ],
                axis=0,
            )
            scores = dot(q_tile, keys, 1, 1) * (score_scale * LOG2E) + mask
            top = jnp.max(scores, axis=-1, keepdims=True)
            raised = jnp.exp2(scores - top)
            total = jnp.sum(raised, axis=-1, keepdims=True)
            probs = raised * (1.0 / total)
            weights = probs.astype(jnp.bfloat16)
            attended = dot(weights, values, 1, 0)
            row_delta = jnp.sum(d_tile.astype(jnp.float32) * attended, axis=-1, keepdims=True)
            grad_probs = dot(d_tile, values, 1, 1)
            grad_scores = (probs * (grad_probs - row_delta)).astype(jnp.bfloat16)
            finished[2, slot, rows, :] = (dot(grad_scores, keys, 1, 0) * score_scale).astype(
                jnp.bfloat16
            )
            key_acc[...] += dot(q_tile, grad_scores, 0, 0)
            value_acc[...] += dot(d_tile, weights, 0, 0)

        finished[0, slot] = (key_acc[...] * score_scale).T.astype(jnp.bfloat16)
        finished[1, slot] = value_acc[...].T.astype(jnp.bfloat16)

        def give_back(step, slot=slot):
            for which in range(3):
                backward(which, slot, step, True).start()

        each_step(give_back)
        for which in range(3):
            own_backward(which, slot).start()

    for slot in range(per_device):

        def drain(step, slot=slot):
            for which in range(4):
                forward(which, slot, step, True).wait_send()
            for which in range(3):
                backward(which, slot, step, True).wait_send()
                backward(which, slot, step, False).wait_recv()

        each_step(drain)
        for which in range(3):
            own_backward(which, slot).wait()


def store_kernel(dq_in, dk_in, dv_in, dq_out, dk_out, dv_out, held, load_sem, store_sem):
    sources = (dq_in, dk_in, dv_in)
    targets = (dq_out, dk_out, dv_out)
    loads = [
        pltpu.make_async_copy(src, held.at[i], load_sem.at[i]) for i, src in enumerate(sources)
    ]
    stores = [
        pltpu.make_async_copy(held.at[i], dst, store_sem.at[i]) for i, dst in enumerate(targets)
    ]
    for load in loads:
        load.start()
    for load, store in zip(loads, stores):
        load.wait()
        store.start()
    for store in stores:
        store.wait()


def whole_head_body(queries, key_rows, value_rows, out_grad, vertical, slash_offsets, counts):
    count = lax.axis_size("seq")
    per_device = HEADS // count
    length = count * BLK
    anywhere = pl.BlockSpec(memory_space=pl.ANY)
    scalars = pl.BlockSpec(memory_space=pltpu.SMEM)
    shape = jax.ShapeDtypeStruct(queries.shape, queries.dtype)
    sems = pltpu.SemaphoreType.DMA
    query_grad, key_grad, value_grad = pl.pallas_call(
        functools.partial(fused_kernel, count, per_device),
        out_shape=(shape, shape, shape),
        in_specs=[anywhere] * 4 + [scalars] * 3,
        out_specs=(anywhere, anywhere, anywhere),
        scratch_shapes=[
            pltpu.VMEM((4, per_device, length, HEAD_DIM), jnp.bfloat16),
            pltpu.VMEM((3, per_device, length, HEAD_DIM), jnp.bfloat16),
            pltpu.VMEM((per_device, count, length), jnp.float32),
            pltpu.VMEM((HEAD_DIM, length), jnp.float32),
            pltpu.VMEM((HEAD_DIM, length), jnp.float32),
            sems((4, per_device, count - 1)),
            sems((4, per_device, count - 1)),
            sems((4, per_device)),
            sems((3, per_device, count - 1)),
            sems((3, per_device, count - 1)),
            sems((3, per_device)),
        ],
        compiler_params=pltpu.CompilerParams(
            collective_id=0, has_side_effects=True, vmem_limit_bytes=64 * 1024 * 1024
        ),
    )(key_rows, value_rows, queries, out_grad, vertical.T, slash_offsets.T, counts.T)
    return pl.pallas_call(
        store_kernel,
        out_shape=(shape, shape, shape),
        in_specs=[anywhere] * 3,
        out_specs=(anywhere,) * 3,
        scratch_shapes=[pltpu.VMEM((3, *shape.shape), shape.dtype), sems((3,)), sems((3,))],
        compiler_params=pltpu.CompilerParams(vmem_limit_bytes=64 * 1024 * 1024),
    )(query_grad, key_grad, value_grad)


def solution(mesh):
    whole_heads = HEADS % mesh.shape["seq"] == 0
    return jax.shard_map(
        whole_head_body if whole_heads else split_head_body,
        mesh=mesh,
        in_specs=(
            P(("doc", "seq"), None),
            P(("doc", "seq"), None),
            P(("doc", "seq"), None),
            P(("doc", "seq"), None),
            P("doc", None),
            P("doc", None),
            P("doc", None),
        ),
        out_specs=(P(("doc", "seq"), None), P(("doc", "seq"), None), P(("doc", "seq"), None)),
        check_vma=False,
    )
```

```python
import functools

import jax
import jax.numpy as jnp
from jax import lax
from jax.experimental import pallas as pl
from jax.experimental.pallas import tpu as pltpu
from jax.sharding import PartitionSpec as P

HEADS = 16
HEAD_DIM = 128
BLK = 128


block_group = 4


def block_lists(chosen, vert_head, slash_head, count_head, nblocks):
    vert_cap = vert_head.shape[0]
    slash_cap = slash_head.shape[0]
    rows_now = chosen.shape[0]
    vert_index = jnp.broadcast_to(vert_head[None, :], (rows_now, vert_cap))
    vert_valid = jnp.broadcast_to(
        (jnp.arange(vert_cap, dtype=jnp.int32) < count_head[0])[None, :], (rows_now, vert_cap)
    )
    slash_index = chosen[:, None] - slash_head[None, :]
    inside = (slash_index >= 0) & (slash_index < nblocks)
    repeated = jnp.any(
        (vert_index[:, :, None] == slash_index[:, None, :]) & vert_valid[:, :, None], axis=1
    )
    slash_valid = (
        (jnp.arange(slash_cap, dtype=jnp.int32) < count_head[1])[None, :]
        & inside
        & jnp.logical_not(repeated)
    )
    index_table = jnp.clip(jnp.concatenate([vert_index, slash_index], axis=1), 0, nblocks - 1)
    valid_table = jnp.concatenate([vert_valid, slash_valid], axis=1)
    return (index_table, valid_table)


def owner_backward(
    q_blocks, k_blocks, v_blocks, d_blocks, vert_head, slash_head, count_head, chosen_all
):
    nblocks, blk_rows, head_dim = q_blocks.shape
    score_scale = head_dim ** (-0.5)
    vert_cap = vert_head.shape[0]
    trips = count_head[0] + count_head[1]

    def one_group(carried, chosen):
        key_acc, value_acc = carried
        index_table, valid_table = block_lists(chosen, vert_head, slash_head, count_head, nblocks)
        q_group = q_blocks[chosen]
        d_group = d_blocks[chosen]
        group_shape = (chosen.shape[0], blk_rows, 1)

        def fetch(position):
            slot_pick = jnp.where(
                position < count_head[0], position, vert_cap + position - count_head[0]
            )
            column = lax.dynamic_index_in_dim(index_table, slot_pick, 1, keepdims=False)
            usable = lax.dynamic_index_in_dim(valid_table, slot_pick, 1, keepdims=False)[
                :, None, None
            ]
            k_tile = k_blocks[column]
            v_tile = v_blocks[column]
            scores = (
                jnp.einsum("gqd,gkd->gqk", q_group, k_tile, preferred_element_type=jnp.float32)
                * score_scale
            )
            return (column, usable, k_tile, v_tile, scores)

        def row_stats(position, running):
            row_top, row_total = running
            column, usable, k_tile, v_tile, scores = fetch(position)
            new_top = jnp.maximum(
                row_top, jnp.where(usable, jnp.max(scores, axis=-1, keepdims=True), -1e30)
            )
            added = jnp.where(
                usable, jnp.sum(jnp.exp(scores - new_top), axis=-1, keepdims=True), 0.0
            )
            return (new_top, row_total * jnp.exp(row_top - new_top) + added)

        row_top, row_total = lax.fori_loop(
            0,
            trips,
            row_stats,
            (jnp.full(group_shape, -1e30, jnp.float32), jnp.zeros(group_shape, jnp.float32)),
        )

        def probs_of(scores, usable):
            return jnp.where(usable, jnp.exp(scores - row_top) / row_total, 0.0)

        def output_step(position, running):
            column, usable, k_tile, v_tile, scores = fetch(position)
            weights = probs_of(scores, usable).astype(jnp.bfloat16)
            return running + jnp.einsum(
                "gqk,gkd->gqd", weights, v_tile, preferred_element_type=jnp.float32
            )

        attended = lax.fori_loop(
            0, trips, output_step, jnp.zeros((chosen.shape[0], blk_rows, head_dim), jnp.float32)
        )
        row_delta = jnp.sum(d_group.astype(jnp.float32) * attended, axis=-1, keepdims=True)

        def grad_step(position, running):
            query_acc, key_run, value_run = running
            column, usable, k_tile, v_tile, scores = fetch(position)
            probs = probs_of(scores, usable)
            weights = probs.astype(jnp.bfloat16)
            grad_probs = jnp.einsum(
                "gqd,gkd->gqk", d_group, v_tile, preferred_element_type=jnp.float32
            )
            grad_scores = (probs * (grad_probs - row_delta)).astype(jnp.bfloat16)
            query_acc = query_acc + jnp.einsum(
                "gqk,gkd->gqd", grad_scores, k_tile, preferred_element_type=jnp.float32
            )
            key_part = (
                jnp.einsum("gqk,gqd->gkd", grad_scores, q_group, preferred_element_type=jnp.float32)
                * score_scale
            )
            value_part = jnp.einsum(
                "gqk,gqd->gkd", weights, d_group, preferred_element_type=jnp.float32
            )
            return (
                query_acc,
                key_run.at[column].add(key_part),
                value_run.at[column].add(value_part),
            )

        start_query = jnp.zeros((chosen.shape[0], blk_rows, head_dim), jnp.float32)
        query_acc, key_acc, value_acc = lax.fori_loop(
            0, trips, grad_step, (start_query, key_acc, value_acc)
        )
        return ((key_acc, value_acc), query_acc * score_scale)

    zeros_acc = jnp.zeros((nblocks, blk_rows, head_dim), jnp.float32)
    (key_acc, value_acc), query_grad = lax.scan(one_group, (zeros_acc, zeros_acc), chosen_all)
    return (query_grad.reshape(-1, blk_rows, head_dim), key_acc, value_acc)


def split_head_body(queries, key_rows, value_rows, out_grad, vertical, slash_offsets, counts):
    tokens_here = queries.shape[0]
    device_count = lax.axis_size("seq")
    device_here = lax.axis_index("seq")
    full_width = HEADS * HEAD_DIM

    def doubled(matrix):
        return jnp.repeat(matrix.reshape(tokens_here, HEADS, HEAD_DIM), 2, axis=1)

    q_owned, k_owned, v_owned, d_owned = (
        lax.all_to_all(doubled(queries), "seq", split_axis=1, concat_axis=0, tiled=True),
        lax.all_to_all(doubled(key_rows), "seq", split_axis=1, concat_axis=0, tiled=True),
        lax.all_to_all(doubled(value_rows), "seq", split_axis=1, concat_axis=0, tiled=True),
        lax.all_to_all(doubled(out_grad), "seq", split_axis=1, concat_axis=0, tiled=True),
    )
    length = tokens_here * device_count
    nblocks = length // BLK
    per_device = 2 * HEADS // device_count
    query_parts = []
    key_parts = []
    value_parts = []
    for local_slot in range(per_device):
        slot_index = device_here * per_device + local_slot
        head_index = slot_index // 2
        parity = slot_index % 2
        chosen_all = (parity + 2 * jnp.arange(nblocks // 2, dtype=jnp.int32)).reshape(
            -1, block_group
        )

        def blockwise(matrix):
            return matrix[:, local_slot, :].reshape(nblocks, BLK, HEAD_DIM)

        query_sel, key_acc, value_acc = owner_backward(
            blockwise(q_owned),
            blockwise(k_owned),
            blockwise(v_owned),
            blockwise(d_owned),
            vertical[head_index],
            slash_offsets[head_index],
            counts[head_index],
            chosen_all,
        )
        query_full = (
            jnp.zeros((nblocks, BLK, HEAD_DIM), jnp.float32)
            .at[chosen_all.reshape(-1)]
            .set(query_sel)
        )
        query_parts.append(query_full.reshape(length, HEAD_DIM))
        key_parts.append(key_acc.reshape(length, HEAD_DIM))
        value_parts.append(value_acc.reshape(length, HEAD_DIM))
    all_parts = (query_parts, key_parts, value_parts)
    stacked = [jnp.stack(member, axis=1) for member in all_parts]
    returned = (
        lax.all_to_all(stacked[0], "seq", split_axis=0, concat_axis=1, tiled=True),
        lax.all_to_all(stacked[1], "seq", split_axis=0, concat_axis=1, tiled=True),
        lax.all_to_all(stacked[2], "seq", split_axis=0, concat_axis=1, tiled=True),
    )
    results = [
        back.reshape(tokens_here, HEADS, 2, HEAD_DIM)
        .sum(axis=2)
        .astype(jnp.bfloat16)
        .reshape(tokens_here, full_width)
        for back in returned
    ]
    return (results[0], results[1], results[2])


MESH = pl.DeviceIdType.MESH
QUERY_TILE = 512
LOG2E = 1.4426950408889634
NEVER = -1e30


def fused_kernel(
    count,
    per_device,
    k_in,
    v_in,
    q_in,
    d_in,
    vertical,
    slash_offsets,
    counts,
    dq_out,
    dk_out,
    dv_out,
    arrived,
    finished,
    bias,
    key_acc,
    value_acc,
    fwd_send,
    fwd_recv,
    fwd_local,
    back_send,
    back_recv,
    back_local,
):
    me = lax.axis_index("seq")
    sources = (k_in, v_in, q_in, d_in)
    targets = (dk_out, dv_out, dq_out)
    length = count * BLK
    score_scale = HEAD_DIM ** (-0.5)

    def offset_of(step):
        return count // 2 + ((step + 1) // 2) * (2 * (step % 2) - 1)

    def rows_of(index):
        return pl.ds(pl.multiple_of(index * BLK, BLK), BLK)

    def columns_of(owner, slot):
        return pl.ds(pl.multiple_of((owner * per_device + slot) * HEAD_DIM, HEAD_DIM), HEAD_DIM)

    def forward(which, slot, step, sending):
        peer = lax.rem(me + offset_of(step), count)
        source = lax.rem(me + count - offset_of(step), count)
        return pltpu.make_async_remote_copy(
            src_ref=sources[which].at[:, columns_of(peer, slot)],
            dst_ref=arrived.at[which, slot, rows_of(me if sending else source), :],
            send_sem=fwd_send.at[which, slot, step],
            recv_sem=fwd_recv.at[which, slot, step],
            device_id={"seq": peer},
            device_id_type=MESH,
        )

    def own_forward(which, slot):
        return pltpu.make_async_copy(
            sources[which].at[:, columns_of(me, slot)],
            arrived.at[which, slot, rows_of(me), :],
            fwd_local.at[which, slot],
        )

    def backward(which, slot, step, sending):
        peer = lax.rem(me + offset_of(step), count)
        source = lax.rem(me + count - offset_of(step), count)
        return pltpu.make_async_remote_copy(
            src_ref=finished.at[which, slot, rows_of(peer), :],
            dst_ref=targets[which].at[:, columns_of(me if sending else source, slot)],
            send_sem=back_send.at[which, slot, step],
            recv_sem=back_recv.at[which, slot, step],
            device_id={"seq": peer},
            device_id_type=MESH,
        )

    def own_backward(which, slot):
        return pltpu.make_async_copy(
            finished.at[which, slot, rows_of(me), :],
            targets[which].at[:, columns_of(me, slot)],
            back_local.at[which, slot],
        )

    def each_step(do):
        @pl.loop(0, count - 1)
        def _(step):
            do(step)

    barrier = pltpu.get_barrier_semaphore()

    @pl.loop(1, count)
    def _(step):
        pl.semaphore_signal(
            barrier, inc=1, device_id={"seq": lax.rem(me + step, count)}, device_id_type=MESH
        )

    pl.semaphore_wait(barrier, count - 1)

    for slot in range(per_device):

        def send_all(step, slot=slot):
            for which in range(4):
                forward(which, slot, step, True).start()

        each_step(send_all)
        for which in range(4):
            own_forward(which, slot).start()

    query_block = lax.broadcasted_iota(jnp.int32, (count, length), 0)
    key_block = lax.broadcasted_iota(jnp.int32, (count, length), 1) // BLK
    for slot in range(per_device):
        head = me * per_device + slot
        allowed = jnp.zeros((count, length), jnp.float32)
        for entry in range(vertical.shape[0]):
            wanted = jnp.where(entry < counts[0, head], vertical[entry, head], -1)
            allowed = jnp.where(key_block == wanted, 1.0, allowed)
        for entry in range(slash_offsets.shape[0]):
            wanted = jnp.where(entry < counts[1, head], slash_offsets[entry, head], 2 * count)
            allowed = jnp.where(query_block - key_block == wanted, 1.0, allowed)
        bias[slot] = jnp.where(allowed > 0.0, 0.0, NEVER)

    def dot(a, b, a_dim, b_dim):
        return lax.dot_general(
            a, b, (((a_dim,), (b_dim,)), ((), ())), preferred_element_type=jnp.float32
        )

    for slot in range(per_device):

        def arrive(step, slot=slot):
            for which in range(4):
                forward(which, slot, step, False).wait_recv()

        each_step(arrive)
        for which in range(4):
            own_forward(which, slot).wait()

        key_acc[...] = jnp.zeros_like(key_acc)
        value_acc[...] = jnp.zeros_like(value_acc)

        @pl.loop(0, length // QUERY_TILE)
        def _(tile, slot=slot):
            rows = pl.ds(pl.multiple_of(tile * QUERY_TILE, QUERY_TILE), QUERY_TILE)
            keys = arrived[0, slot]
            values = arrived[1, slot]
            q_tile = arrived[2, slot, rows, :]
            d_tile = arrived[3, slot, rows, :]
            blocks_here = QUERY_TILE // BLK
            mask = jnp.concatenate(
                [
                    jnp.broadcast_to(
                        bias[slot, pl.ds(tile * blocks_here + part, 1), :], (BLK, length)
                    )
                    for part in range(blocks_here)
                ],
                axis=0,
            )
            scores = dot(q_tile, keys, 1, 1) * (score_scale * LOG2E) + mask
            top = jnp.max(scores, axis=-1, keepdims=True)
            raised = jnp.exp2(scores - top)
            total = jnp.sum(raised, axis=-1, keepdims=True)
            probs = raised * (1.0 / total)
            weights = probs.astype(jnp.bfloat16)
            attended = dot(weights, values, 1, 0)
            row_delta = jnp.sum(d_tile.astype(jnp.float32) * attended, axis=-1, keepdims=True)
            grad_probs = dot(d_tile, values, 1, 1)
            grad_scores = (probs * (grad_probs - row_delta)).astype(jnp.bfloat16)
            finished[2, slot, rows, :] = (dot(grad_scores, keys, 1, 0) * score_scale).astype(
                jnp.bfloat16
            )
            key_acc[...] += dot(q_tile, grad_scores, 0, 0)
            value_acc[...] += dot(d_tile, weights, 0, 0)

        finished[0, slot] = (key_acc[...] * score_scale).T.astype(jnp.bfloat16)
        finished[1, slot] = value_acc[...].T.astype(jnp.bfloat16)

        def give_back(step, slot=slot):
            for which in range(3):
                backward(which, slot, step, True).start()

        each_step(give_back)
        for which in range(3):
            own_backward(which, slot).start()

    for slot in range(per_device):

        def drain(step, slot=slot):
            for which in range(4):
                forward(which, slot, step, True).wait_send()
            for which in range(3):
                backward(which, slot, step, True).wait_send()
                backward(which, slot, step, False).wait_recv()

        each_step(drain)
        for which in range(3):
            own_backward(which, slot).wait()


def store_kernel(dq_in, dk_in, dv_in, dq_out, dk_out, dv_out, held, load_sem, store_sem):
    sources = (dq_in, dk_in, dv_in)
    targets = (dq_out, dk_out, dv_out)
    loads = [
        pltpu.make_async_copy(src, held.at[i], load_sem.at[i]) for i, src in enumerate(sources)
    ]
    stores = [
        pltpu.make_async_copy(held.at[i], dst, store_sem.at[i]) for i, dst in enumerate(targets)
    ]
    for load in loads:
        load.start()
    for load, store in zip(loads, stores):
        load.wait()
        store.start()
    for store in stores:
        store.wait()


def whole_head_body(queries, key_rows, value_rows, out_grad, vertical, slash_offsets, counts):
    count = lax.axis_size("seq")
    per_device = HEADS // count
    length = count * BLK
    anywhere = pl.BlockSpec(memory_space=pl.ANY)
    scalars = pl.BlockSpec(memory_space=pltpu.SMEM)
    shape = jax.ShapeDtypeStruct(queries.shape, queries.dtype)
    sems = pltpu.SemaphoreType.DMA
    query_grad, key_grad, value_grad = pl.pallas_call(
        functools.partial(fused_kernel, count, per_device),
        out_shape=(shape, shape, shape),
        in_specs=[anywhere] * 4 + [scalars] * 3,
        out_specs=(anywhere, anywhere, anywhere),
        scratch_shapes=[
            pltpu.VMEM((4, per_device, length, HEAD_DIM), jnp.bfloat16),
            pltpu.VMEM((3, per_device, length, HEAD_DIM), jnp.bfloat16),
            pltpu.VMEM((per_device, count, length), jnp.float32),
            pltpu.VMEM((HEAD_DIM, length), jnp.float32),
            pltpu.VMEM((HEAD_DIM, length), jnp.float32),
            sems((4, per_device, count - 1)),
            sems((4, per_device, count - 1)),
            sems((4, per_device)),
            sems((3, per_device, count - 1)),
            sems((3, per_device, count - 1)),
            sems((3, per_device)),
        ],
        compiler_params=pltpu.CompilerParams(
            collective_id=0, has_side_effects=True, vmem_limit_bytes=64 * 1024 * 1024
        ),
    )(key_rows, value_rows, queries, out_grad, vertical.T, slash_offsets.T, counts.T)
    return pl.pallas_call(
        store_kernel,
        out_shape=(shape, shape, shape),
        in_specs=[anywhere] * 3,
        out_specs=(anywhere,) * 3,
        scratch_shapes=[pltpu.VMEM((3, *shape.shape), shape.dtype), sems((3,)), sems((3,))],
        compiler_params=pltpu.CompilerParams(vmem_limit_bytes=64 * 1024 * 1024),
    )(query_grad, key_grad, value_grad)


def solution(mesh):
    whole_heads = HEADS % mesh.shape["seq"] == 0
    return jax.shard_map(
        whole_head_body if whole_heads else split_head_body,
        mesh=mesh,
        in_specs=(
            P(("doc", "seq"), None),
            P(("doc", "seq"), None),
            P(("doc", "seq"), None),
            P(("doc", "seq"), None),
            P("doc", None),
            P("doc", None),
            P("doc", None),
        ),
        out_specs=(P(("doc", "seq"), None), P(("doc", "seq"), None), P(("doc", "seq"), None)),
        check_vma=False,
    )
```
